512 devices in a mesh: row: 32 (over z_lo, y), col: 16 (over z_hi, x, core).
Axes of the slice: x: 4, y: 4, z: 16 (z_hi: 2, z_lo: 8; z = z_hi * 8 + z_lo), core: 2. Of those that a mesh axis runs over, the one named last changes fastest.
Arguments:
- entries: int32 [128, 64, 128, 128], P('row', 'col'), may hold values from -2 to 2
- tile_cols: int32 [128, 64], P('row', 'col'), may hold values from 0 to 31
- block_now: int32 [32, 65536], P(None, ('col', 'row')), may hold values from 0 to 65520
- block_prev: int32 [32, 65536], P(None, ('col', 'row')), may hold values from 0 to 65520
- block_prev2: int32 [32, 65536], P(None, ('col', 'row')), may hold values from 0 to 65520
- gram_prev: int32 [32, 32], replicated, may hold values from 0 to 65520
- square_prev: int32 [32, 32], replicated, may hold values from 0 to 65520
- inverse_prev: int32 [32, 32], replicated, may hold values from 0 to 65520
- inverse_prev2: int32 [32, 32], replicated, may hold values from 0 to 65520
Outputs:
- next_block: float32 [32, 65536], P(None, ('col', 'row'))
- later_block: float32 [32, 65536], P(None, ('col', 'row'))
The draws below stay inside these ranges and needn't reach their ends.
Inputs may be any that keep to these rules, and one draw needn't show every extreme that they name: `tile_cols`: stored tiles that name the same tile column in one tile row add. `block_prev`: residues. `block_prev2`: residues. `gram_prev`: residues. `square_prev`: residues. `inverse_prev`: residues. `inverse_prev2`: residues.
All inputs are finite; a program needn't handle non-finite values.
Results may differ from the reference program's by a relative error of at most 0.0003.
Values sent between devices are 32-bit elements; how exact they have to be, the bound alone decides.
No kernel may reach another device: no remote copies, remote signals or barrier semaphores. Data moves between devices by JAX's collectives and lax.ppermute only.
A program may use at most 64 MiB of HBM per device.

```python
import jax
import jax.numpy as jnp
from jax import lax

BLOCK = 32
TILE = 128
SLOTS = 4
TCOLS = 32
ORDER = 65536
TROWS_ALL = 128
SLOTS_ALL = 64
N_COL = 16


def with_ends(values, key, least, top_value):
    extent = values.shape
    index_at = [jax.random.randint(jax.random.fold_in(key, axis), (), 0, extent[axis]) for axis in range(len(extent))]
    values = values.at[tuple(index_at)].set(least)
    longest = extent.index(max(extent))
    index_at[longest] = (index_at[longest] + 1) % extent[longest]
    return values.at[tuple(index_at)].set(top_value)


def setup_inputs(seed: int = 0) -> dict:
    seeds = jax.random.split(jax.random.key(seed), 10)
    return {
        "entries": with_ends(jax.random.randint(seeds[0], (TROWS_ALL, SLOTS_ALL, TILE, TILE), -2, 3), jax.random.fold_in(seeds[0], 1), -2, 2).astype(jnp.int32),
        "tile_cols": with_ends(jax.random.randint(seeds[1], (TROWS_ALL, SLOTS_ALL), 0, TCOLS), jax.random.fold_in(seeds[1], 1), 0, TCOLS - 1).astype(jnp.int32),
        "block_now": with_ends(jax.random.randint(seeds[2], (BLOCK, ORDER), 0, 65521), jax.random.fold_in(seeds[2], 1), 0, 65520).astype(jnp.int32),
        "block_prev": with_ends(jax.random.randint(seeds[3], (BLOCK, ORDER), 0, 65521), jax.random.fold_in(seeds[3], 1), 0, 65520).astype(jnp.int32),
        "block_prev2": with_ends(jax.random.randint(seeds[4], (BLOCK, ORDER), 0, 65521), jax.random.fold_in(seeds[4], 1), 0, 65520).astype(jnp.int32),
        "gram_prev": with_ends(jax.random.randint(seeds[5], (BLOCK, BLOCK), 0, 65521), jax.random.fold_in(seeds[5], 1), 0, 65520).astype(jnp.int32),
        "square_prev": with_ends(jax.random.randint(seeds[6], (BLOCK, BLOCK), 0, 65521), jax.random.fold_in(seeds[6], 1), 0, 65520).astype(jnp.int32),
        "inverse_prev": with_ends(jax.random.randint(seeds[7], (BLOCK, BLOCK), 0, 65521), jax.random.fold_in(seeds[7], 1), 0, 65520).astype(jnp.int32),
        "inverse_prev2": with_ends(jax.random.randint(seeds[8], (BLOCK, BLOCK), 0, 65521), jax.random.fold_in(seeds[8], 1), 0, 65520).astype(jnp.int32),
    }


modulus = 65521.0


def residue(values):
    return jnp.mod(values, modulus)


def split_digits(values):
    top_part = jnp.floor(values / 256.0)
    return top_part, values - top_part * 256.0


def fold_digits(top_sum, low_sum):
    return residue(residue(residue(top_sum) * 256.0) + residue(low_sum))


def fold_three(upper_part, middle, lower_part):
    return residue(residue(residue(upper_part) * 15.0) + residue(residue(middle) * 256.0) + residue(lower_part))


def mulmod(left_side, right_side):
    top_part, low_part = split_digits(right_side)
    return fold_digits(left_side * top_part, left_side * low_part)


def exact_dot(left_side, right_side):
    return jnp.dot(left_side, right_side, precision=lax.Precision.HIGHEST, preferred_element_type=jnp.float32)


def small_product(left_side, right_side):
    left_top, left_low = split_digits(left_side)
    right_top, right_low = split_digits(right_side)
    return fold_three(exact_dot(left_top, right_top), exact_dot(left_top, right_low) + exact_dot(left_low, right_top), exact_dot(left_low, right_low))


def inverse_scalar(number):
    result = jnp.ones_like(number)
    square = number
    exponent = 65519
    for position in range(16):
        if (exponent >> position) & 1:
            result = mulmod(result, square)
        square = mulmod(square, square)
    return result


def inverse_matrix(matrix):
    matrix_order = matrix.shape[0]
    augmented = jnp.concatenate([matrix, jnp.eye(matrix_order, dtype=matrix.dtype)], axis=1)
    row_numbers = jnp.arange(matrix_order, dtype=jnp.int32)

    def eliminate(column, augmented):
        column = jnp.asarray(column).astype(jnp.int32)
        pivot_column = augmented[:, column]
        usable = (pivot_column != 0.0) & (row_numbers >= column)
        pivot_row_id = jnp.where(jnp.any(usable), jnp.argmax(usable).astype(jnp.int32), column)
        pivot_row = augmented[pivot_row_id]
        current_row = augmented[column]
        swapped = jnp.where((row_numbers == column)[:, None], pivot_row[None, :], jnp.where((row_numbers == pivot_row_id)[:, None], current_row[None, :], augmented))
        scaled = mulmod(pivot_row, inverse_scalar(pivot_row[column]))
        factors = jnp.where(row_numbers == column, 0.0, swapped[:, column])
        reduced = residue(swapped - mulmod(factors[:, None], scaled[None, :]) + modulus)
        return jnp.where((row_numbers == column)[:, None], scaled[None, :], reduced)

    augmented = lax.fori_loop(0, matrix_order, eliminate, augmented)
    return augmented[:, matrix_order:]


def coefficients(gram_now, square_now, inverse_now, inverse_prev, inverse_prev2, gram_old, square_old):
    identity = jnp.eye(gram_now.shape[0], dtype=gram_now.dtype)
    first = residue(identity - small_product(residue(square_now + gram_now), inverse_now) + modulus)
    second = residue(modulus - small_product(gram_now, inverse_prev))
    middle = residue(identity - small_product(inverse_prev, gram_old) + modulus)
    third = residue(modulus - small_product(small_product(residue(square_old + gram_old), middle), inverse_prev2))
    return jnp.concatenate([first, second, third], axis=1)


def combine_blocks(coeffs, stacked):
    coeff_top, coeff_low = split_digits(coeffs)
    stack_top, stack_low = split_digits(stacked)
    left_side = jnp.stack([coeff_top, coeff_low])
    right_side = jnp.stack([stack_top, stack_low])
    products = jnp.einsum('dab,ebn->dean', left_side, right_side, precision=lax.Precision.HIGHEST)
    return fold_three(products[0, 0], products[0, 1] + products[1, 0], products[1, 1])


def gram_whole(first, second):
    column_count = first.shape[1]
    group_width = min(column_count, 128)
    groups = column_count // group_width
    first_digits = jnp.stack(split_digits(first)).reshape(2, first.shape[0], groups, group_width)
    second_digits = jnp.stack(split_digits(second)).reshape(2, second.shape[0], groups, group_width)
    products = jnp.einsum('dagw,ecgw->gdeac', first_digits, second_digits, precision=lax.Precision.HIGHEST)
    per_group = fold_three(products[:, 0, 0], products[:, 0, 1] + products[:, 1, 0], products[:, 1, 1])
    top_part, low_part = split_digits(per_group)
    return fold_digits(jnp.sum(top_part, axis=0), jnp.sum(low_part, axis=0))


def reference(entries, tile_cols, block_now, block_prev, block_prev2, gram_prev, square_prev, inverse_prev, inverse_prev2):
    col_tiles = TCOLS * N_COL
    slot_owner = (jnp.arange(SLOTS * N_COL, dtype=jnp.int32) // SLOTS) * TCOLS
    global_cols = (tile_cols + slot_owner[None, :]).astype(jnp.int32)

    def apply_operator(block):
        top_part, low_part = split_digits(block)
        digits = jnp.concatenate([top_part, low_part], axis=0).reshape(2 * BLOCK, col_tiles, TILE)

        def per_row(running, inputs):
            tile_row, cols_row = inputs
            matrix = tile_row.astype(jnp.float32)
            picked = jnp.take(digits, cols_row, axis=1)
            raw_sums = jnp.einsum('bsk,sjk->bj', picked, matrix, precision=lax.Precision.HIGHEST)
            projected = fold_digits(raw_sums[:BLOCK], raw_sums[BLOCK:])
            proj_top, proj_low = split_digits(projected)
            proj_digits = jnp.concatenate([proj_top, proj_low], axis=0)
            spread = jnp.einsum('bj,sjk->bsk', proj_digits, matrix, precision=lax.Precision.HIGHEST)
            per_slot = fold_digits(spread[:BLOCK], spread[BLOCK:])
            return residue(running.at[:, cols_row, :].add(per_slot)), None

        totals, unused = lax.scan(per_row, jnp.zeros((BLOCK, col_tiles, TILE), jnp.float32), (entries, global_cols))
        return totals.reshape(BLOCK, col_tiles * TILE)

    current = block_now.astype(jnp.float32)
    earlier = block_prev.astype(jnp.float32)
    earliest = block_prev2.astype(jnp.float32)
    gram_old = gram_prev.astype(jnp.float32)
    square_old = square_prev.astype(jnp.float32)
    inverse_old = inverse_prev.astype(jnp.float32)
    inverse_older = inverse_prev2.astype(jnp.float32)
    results = []
    for iteration in range(2):
        applied = apply_operator(current)
        gram_now = gram_whole(current, applied)
        square_now = gram_whole(applied, applied)
        inverse_now = inverse_matrix(gram_now)
        coeffs = coefficients(gram_now, square_now, inverse_now, inverse_old, inverse_older, gram_old, square_old)
        stacked = jnp.concatenate([current, earlier, earliest], axis=0)
        following = residue(applied + combine_blocks(coeffs, stacked))
        results.append(following / modulus)
        earliest, earlier, current = earlier, current, following
        inverse_older, inverse_old = inverse_old, inverse_now
        gram_old, square_old = gram_now, square_now
    return results[0], results[1]
```

```python
import functools

import jax
import jax.numpy as jnp
from jax import lax
from jax.experimental import pallas as pl
from jax.experimental.pallas import tpu as pltpu
from jax.sharding import Mesh
from jax.sharding import PartitionSpec as P

PRIME = 65521
modulus = 65521.0
BLOCK = 32
TILE = 128
ROW_Z, ROW_Y = 8, 4
COL_Z, COL_X, COL_C = 2, 4, 2
ROWS = ROW_Z * ROW_Y
SMALL = 8
PART = ROW_Z * BLOCK

f32, bf16, i32 = jnp.float32, jnp.bfloat16, jnp.int32


def modp(x):
    top = jnp.floor(x * (1.0 / 65536.0))
    rest = x - top * modulus
    return jnp.where(rest >= modulus, rest - modulus, rest)


def digits(x):
    top = jnp.floor(x * (1.0 / 256.0))
    return top, x - top * 256.0


def stack_digits(x):
    top, low = digits(x)
    return jnp.concatenate([top, low], axis=0).astype(bf16)


def fold_two(top, low):
    return modp(modp(modp(top) * 256.0) + low)


def fold_three(upper, middle, lower):
    return modp(modp(upper) * 15.0 + modp(modp(middle) * 256.0) + lower)


def dot(a, b):
    return lax.dot_general(a, b, (((1,), (0,)), ((), ())), preferred_element_type=f32)


def dot_t(a, b):
    return lax.dot_general(a, b, (((1,), (1,)), ((), ())), preferred_element_type=f32)


def product(left, right):
    stacked = stack_digits(left)
    top, low = digits(right)
    by_top = dot(stacked, top.astype(bf16))
    by_low = dot(stacked, low.astype(bf16))
    return fold_three(by_top[:BLOCK], by_top[BLOCK:] + by_low[:BLOCK], by_low[BLOCK:])


def self_product(stacked):
    all_four = dot_t(stacked, stacked)
    by_top = all_four[:, :BLOCK]
    by_low = all_four[:, BLOCK:]
    return fold_three(by_top[:BLOCK], by_top[BLOCK:] + by_low[:BLOCK], by_low[BLOCK:])


def pack(matrix):
    return jnp.concatenate([matrix[8 * k : 8 * k + 8] for k in range(4)], axis=1)


def unpack(packed):
    return jnp.concatenate([packed[:, 32 * k : 32 * k + 32] for k in range(4)], axis=0)


def eye():
    rows = lax.broadcasted_iota(i32, (BLOCK, BLOCK), 0)
    cols = lax.broadcasted_iota(i32, (BLOCK, BLOCK), 1)
    return (rows == cols).astype(f32)


def shrink(x):
    return lax.shift_right_logical(x, 16) * 15 + (x & 65535)


def settle(x):
    return jnp.where(x >= PRIME, x - PRIME, x)


def mulmod(a, b):
    return settle(shrink(shrink(a * b)))


def power(a):
    def fourth_up(x):
        for unused in range(4):
            x = mulmod(x, x)
        return x

    a2 = mulmod(a, a)
    a3 = mulmod(a2, a)
    a6 = mulmod(a3, a3)
    a12 = mulmod(a6, a6)
    a14 = mulmod(a12, a2)
    a15 = mulmod(a12, a3)
    a255 = mulmod(fourth_up(a15), a15)
    high = mulmod(fourth_up(a255), a14)
    return mulmod(fourth_up(high), a15)


def to_int(x):
    return x.astype(i32)


def lane_sum(x):
    return to_int(jnp.sum(x.astype(f32), axis=1, keepdims=True))


def sublane_sum(x):
    return to_int(jnp.sum(x.astype(f32), axis=0, keepdims=True))


def invert(gram, out_ref):
    wide = (BLOCK, 128)
    rows = lax.broadcasted_iota(i32, wide, 0)
    lanes = lax.broadcasted_iota(i32, wide, 1)
    start = jnp.concatenate([gram, eye(), jnp.zeros((BLOCK, 64), f32)], axis=1)
    start = to_int(start)

    matrix = start
    least = jnp.full((1, 1), PRIME, i32)
    for c in range(BLOCK):
        pivot_row = matrix[c : c + 1, :]
        pivot = matrix[c : c + 1, c : c + 1]
        column = matrix[:, c : c + 1]
        least = jnp.minimum(least, pivot)
        kept = shrink(matrix * jnp.broadcast_to(pivot, wide))
        taken = shrink(jnp.broadcast_to(column, wide) * jnp.broadcast_to(pivot_row, wide))
        updated = settle(shrink(kept - taken + 17 * PRIME))
        matrix = jnp.where(rows == c, matrix, updated)
    diagonal = lane_sum(jnp.where(rows == lanes, matrix, 0))
    scale = power(jnp.broadcast_to(diagonal, wide))
    out_ref[...] = mulmod(matrix, scale)[:, BLOCK : 2 * BLOCK].astype(f32)

    @pl.when(jnp.min(least.astype(f32)) == 0.0)
    def _():
        def eliminate(c, m):
            column = lane_sum(jnp.where(lanes == c, m, 0))
            row_ids = lax.broadcasted_iota(i32, (BLOCK, 1), 0)
            usable = (column != 0) & (row_ids >= c)
            at = jnp.min(jnp.where(usable, row_ids, BLOCK).astype(f32), axis=0, keepdims=True)
            at = to_int(at)
            at = jnp.where(at == BLOCK, c, at)
            at = jnp.broadcast_to(at, wide)
            pivot_row = jnp.broadcast_to(sublane_sum(jnp.where(rows == at, m, 0)), wide)
            current = jnp.broadcast_to(sublane_sum(jnp.where(rows == c, m, 0)), wide)
            swapped = jnp.where(rows == c, pivot_row, jnp.where(rows == at, current, m))
            pivot = jnp.broadcast_to(lane_sum(jnp.where(lanes == c, pivot_row, 0)), wide)
            scaled = mulmod(pivot_row, power(pivot))
            factors = jnp.broadcast_to(lane_sum(jnp.where(lanes == c, swapped, 0)), wide)
            reduced = settle(swapped - mulmod(factors, scaled) + PRIME)
            return jnp.where(rows == c, scaled, reduced)

        m = lax.fori_loop(0, BLOCK, eliminate, start)
        out_ref[...] = m[:, BLOCK : 2 * BLOCK].astype(f32)


def call(kernel, outs, args, smem=(), scratch=(), flops=0):
    specs = [
        pl.BlockSpec(memory_space=pltpu.SMEM if n in smem else pltpu.VMEM)
        for n in range(len(args))
    ]
    shapes = [jax.ShapeDtypeStruct(s, t) for s, t in outs]
    got = pl.pallas_call(
        kernel,
        out_shape=shapes,
        in_specs=specs,
        out_specs=[pl.BlockSpec(memory_space=pltpu.VMEM)] * len(shapes),
        scratch_shapes=list(scratch),
        compiler_params=pltpu.CompilerParams(vmem_limit_bytes=32 * 2**20),
        cost_estimate=pl.CostEstimate(flops=flops, bytes_accessed=4 * 2**20, transcendentals=0),
    )(*args)
    return got


def tile_at(t):
    return lax.rem(t, ROW_Y), lax.div(t, ROW_Y) * BLOCK


def forward(cols_ref, block_ref, tiles_ref, out_ref, count, slots):
    for r in range(count):
        total = None
        for s in range(slots):
            part, row = tile_at(cols_ref[r, s])
            picked = block_ref[part, pl.ds(pl.multiple_of(row, BLOCK), BLOCK), :]
            term = dot_t(stack_digits(picked), tiles_ref[r * slots + s])
            total = term if total is None else total + term
        out_ref[r * BLOCK : (r + 1) * BLOCK, :] = fold_two(total[:BLOCK], total[BLOCK:])


def backward(cols_ref, projected, tiles_ref, sums_ref, out_ref, count, slots):
    sums_ref[...] = jnp.zeros_like(sums_ref)
    gram = jnp.zeros((BLOCK, BLOCK), f32)
    for r in range(count):
        stacked = stack_digits(projected[r])
        gram = gram + self_product(stacked)
        for s in range(slots):
            t = cols_ref[r, s]
            sums_ref[t] += dot(stacked, tiles_ref[r * slots + s])
    for t in range(ROWS):
        whole = sums_ref[t]
        y, z = t % ROW_Y, t // ROW_Y
        out_ref[y, z * BLOCK : (z + 1) * BLOCK, :] = fold_two(whole[:BLOCK], whole[BLOCK:])
    packed = pack(modp(gram))
    for y in range(ROW_Y):
        out_ref[y, PART : PART + SMALL, :] = packed


def forward_first_kernel(count, slots, cols_ref, block_ref, tiles_ref, out_ref):
    forward(cols_ref, block_ref, tiles_ref, out_ref, count, slots)


def forward_second_kernel(count, slots, cols_ref, block_ref, tiles_ref, out_ref):
    forward(cols_ref, block_ref, tiles_ref, out_ref, count, slots)
    square = block_ref[0, PART : PART + SMALL, :]
    for y in range(1, ROW_Y):
        square = square + block_ref[y, PART : PART + SMALL, :]
    out_ref[count * BLOCK : count * BLOCK + SMALL, :] = modp(square)


def backward_first_kernel(count, slots, cols_ref, own_ref, other_ref, tiles_ref, out_ref, y_ref, sums_ref):
    projected = []
    for r in range(count):
        at = slice(r * BLOCK, (r + 1) * BLOCK)
        value = modp(own_ref[at, :] + other_ref[at, :])
        y_ref[at, :] = value
        projected.append(value)
    backward(cols_ref, projected, tiles_ref, sums_ref, out_ref, count, slots)


def backward_second_kernel(
    count, slots, cols_ref, own_ref, other_ref, tiles_ref, gram_ref, inv_y_ref, inv_x_ref, old_ref, shifted_ref,
    out_ref, next_ref, result_ref, third_ref, sums_ref,
):
    small = slice(count * BLOCK, count * BLOCK + SMALL)
    square = unpack(modp(own_ref[small, :] + other_ref[small, :]))
    both = modp(square + gram_ref[...])
    projected = []
    for r in range(count):
        at = slice(r * BLOCK, (r + 1) * BLOCK)
        value = modp(own_ref[at, :] + other_ref[at, :])
        projected.append(modp(value - product(both, inv_y_ref[at, :]) + modulus))
    backward(cols_ref, projected, tiles_ref, sums_ref, out_ref, count, slots)
    following = modp(shifted_ref[...] - product(both, inv_x_ref[...]) + modulus)
    next_ref[...] = following
    result_ref[...] = following / modulus
    third_ref[...] = product(both, old_ref[...])


def sum_y_kernel(in_ref, out_ref):
    for z in range(ROW_Z):
        at = slice(z * BLOCK, (z + 1) * BLOCK)
        total = in_ref[0, at, :]
        for y in range(1, ROW_Y):
            total = total + in_ref[y, at, :]
        out_ref[z, :BLOCK, :] = total
    small = slice(PART, PART + SMALL)
    total = in_ref[0, small, :]
    for y in range(1, ROW_Y):
        total = total + in_ref[y, small, :]
    for z in range(ROW_Z):
        out_ref[z, BLOCK:, :] = total


def summed(in_ref):
    total = in_ref[0]
    for k in range(1, in_ref.shape[0]):
        total = total + in_ref[k]
    return modp(total)


def third_kernel(gram_ref, square_ref, inverse_ref, older_ref, now_ref, earliest_ref, out_ref):
    gram = gram_ref[...]
    middle = modp(eye() - product(inverse_ref[...], gram) + modulus)
    third = product(product(modp(square_ref[...] + gram), middle), older_ref[...])
    out_ref[...] = modp(now_ref[...] - product(third, earliest_ref[...]) + modulus)


def shift_kernel(in_ref, inverse_ref, earlier_ref, base_ref, out_ref, shifted_ref, gram_ref):
    total = summed(in_ref)
    applied = total[:BLOCK]
    gram = unpack(total[BLOCK:])
    gram_ref[...] = gram
    second = product(gram, inverse_ref[...])
    shifted = modp(applied + base_ref[...] + (modulus - product(second, earlier_ref[...])))
    shifted_ref[...] = shifted
    square = pack(self_product(stack_digits(applied)))
    for z in range(ROW_Z):
        out_ref[z, :BLOCK, :] = shifted
        out_ref[z, BLOCK:, :] = square


def spread_y_kernel(in_ref, out_ref):
    square = in_ref[0, BLOCK:, :]
    for z in range(1, ROW_Z):
        square = square + in_ref[z, BLOCK:, :]
    square = modp(square)
    for y in range(ROW_Y):
        for z in range(ROW_Z):
            out_ref[y, z * BLOCK : (z + 1) * BLOCK, :] = in_ref[z, :BLOCK, :]
        out_ref[y, PART:, :] = square


def inverse_kernel(
    count, gram_ref, older_ref, y_ref, now_ref, earlier_ref, inv_y_ref, inv_x_ref, old_ref, inverse_ref
):
    gram = gram_ref[...]
    invert(gram, inverse_ref)
    inverse = inverse_ref[...]
    for r in range(count):
        at = slice(r * BLOCK, (r + 1) * BLOCK)
        inv_y_ref[at, :] = product(inverse, y_ref[at, :])
    inv_x_ref[...] = product(inverse, now_ref[...])
    middle = modp(eye() - product(inverse, gram) + modulus)
    old_ref[...] = product(product(middle, older_ref[...]), earlier_ref[...])


def ending_kernel(in_ref, next_ref, inv_x_ref, third_ref, out_ref, base_ref, inv_next_ref, gram_ref, inverse_ref):
    total = summed(in_ref)
    applied = total[:BLOCK]
    gram = unpack(total[BLOCK:])
    gram_ref[...] = gram
    square = pack(self_product(stack_digits(applied)))
    for k in range(out_ref.shape[0]):
        out_ref[k] = square
    following = next_ref[...]
    minus = modp(product(gram, inv_x_ref[...]) + third_ref[...])
    base_ref[...] = modp(applied + following + (modulus - minus))
    invert(gram, inverse_ref)
    inv_next_ref[...] = product(inverse_ref[...], following)


def relay_kernel(in_ref, out_ref):
    total = summed(in_ref)
    for k in range(out_ref.shape[0]):
        out_ref[k] = total


def last_kernel(in_ref, gram_ref, base_ref, inv_next_ref, out_ref):
    both = modp(unpack(summed(in_ref)) + gram_ref[...])
    out_ref[...] = modp(base_ref[...] - product(both, inv_next_ref[...]) + modulus) / modulus


def exchange(parts, axis):
    return lax.all_to_all(parts, axis, 0, 0, tiled=True)


def flip(x, axis):
    return lax.ppermute(x, axis, [(0, 1), (1, 0)])


def sum_core_x(partial):
    pair = partial + flip(partial, "c")
    return jnp.sum(exchange(jnp.broadcast_to(pair[None], (COL_X, *pair.shape)), "x"), axis=0)


def body(entries, tile_cols, block_now, block_prev, block_prev2, gram_prev, square_prev, inverse_prev, inverse_prev2):
    count, slots = tile_cols.shape
    length = count * BLOCK
    tiles = entries.astype(bf16).reshape(count * slots, TILE, TILE)
    current, earlier, earliest = (b.astype(f32) for b in (block_now, block_prev, block_prev2))
    gram_old, square_old, inverse_old, inverse_older = (
        m.astype(f32) for m in (gram_prev, square_prev, inverse_prev, inverse_prev2)
    )
    shard = (BLOCK, TILE)
    small = (BLOCK, BLOCK)
    sums = [pltpu.VMEM((ROWS, 2 * BLOCK, TILE), f32)]

    along_z = exchange(jnp.broadcast_to(current[None], (ROW_Z, *shard)), "zl")
    block = exchange(jnp.broadcast_to(along_z.reshape(1, PART, TILE), (ROW_Y, PART, TILE)), "y")
    [partial] = call(
        functools.partial(forward_first_kernel, count, slots), [((length, TILE), f32)], [tile_cols, block, tiles], smem=(0,)
    )
    own = sum_core_x(partial)
    other = flip(own, "zh")
    [base] = call(
        third_kernel, [(shard, f32)],
        [gram_old, square_old, inverse_old, inverse_older, current, earliest],
        flops=10**9,
    )

    spread, projected = call(
        functools.partial(backward_first_kernel, count, slots),
        [((ROW_Y, PART + SMALL, TILE), f32), ((length, TILE), f32)],
        [tile_cols, own, other, tiles], smem=(0,), scratch=sums,
    )
    chunks = (ROW_Z, BLOCK + SMALL, TILE)
    [by_z] = call(sum_y_kernel, [(chunks, f32)], [exchange(spread, "y")])
    out, shifted, gram_now = call(
        shift_kernel, [(chunks, f32), (shard, f32), (small, f32)],
        [exchange(by_z, "zl"), inverse_old, earlier, base],
    )

    [spread] = call(spread_y_kernel, [((ROW_Y, PART + SMALL, TILE), f32)], [exchange(out, "zl")])
    [partial] = call(
        functools.partial(forward_second_kernel, count, slots),
        [((length + SMALL, TILE), f32)], [tile_cols, exchange(spread, "y"), tiles], smem=(0,),
    )
    own = sum_core_x(partial)
    other = flip(own, "zh")
    inv_y, inv_x, old, inverse_now = call(
        functools.partial(inverse_kernel, count),
        [((length, TILE), f32), (shard, f32), (shard, f32), (small, f32)],
        [gram_now, inverse_old, projected, current, earlier],
        flops=10**9,
    )
    spread, following, result, third = call(
        functools.partial(backward_second_kernel, count, slots),
        [((ROW_Y, PART + SMALL, TILE), f32), (shard, f32), (shard, f32), (shard, f32)],
        [tile_cols, own, other, tiles, gram_now, inv_y, inv_x, old, shifted], smem=(0,), scratch=sums,
    )
    [by_z] = call(sum_y_kernel, [(chunks, f32)], [exchange(spread, "y")])
    near = ROW_Y * COL_X * COL_C
    far = COL_Z * ROW_Z
    out, base, inv_next, gram_next, inverse_next = call(
        ending_kernel,
        [((near, SMALL, TILE), f32), (shard, f32), (shard, f32), (small, f32), (small, f32)],
        [exchange(by_z, "zl"), following, inv_x, third],
    )
    [out] = call(relay_kernel, [((far, SMALL, TILE), f32)], [exchange(out, ("y", "x", "c"))])
    [later] = call(last_kernel, [(shard, f32)], [exchange(out, ("zh", "zl")), gram_next, base, inv_next])
    return result, later


def solution(mesh):
    fine = Mesh(mesh.devices.reshape(ROW_Z, ROW_Y, COL_Z, COL_X, COL_C), ("zl", "y", "zh", "x", "c"))
    row, col = ("zl", "y"), ("zh", "x", "c")
    columns = P(None, (*col, *row))
    return jax.shard_map(
        body,
        mesh=fine,
        in_specs=(P(row, col, None, None), P(row, col), columns, columns, columns, P(), P(), P(), P()),
        out_specs=(columns, columns),
        check_vma=False,
    )
```

```python
import functools

import jax
import jax.numpy as jnp
from jax import lax
from jax.experimental import pallas as pl
from jax.experimental.pallas import tpu as pltpu
from jax.sharding import Mesh
from jax.sharding import PartitionSpec as P

PRIME = 65521
modulus = 65521.0
BLOCK = 32
TILE = 128
ROW_Z, ROW_Y = 8, 4
COL_Z, COL_X, COL_C = 2, 4, 2
ROWS = ROW_Z * ROW_Y
SMALL = 8
PART = ROW_Z * BLOCK

f32, bf16, i32 = jnp.float32, jnp.bfloat16, jnp.int32


def modp(x):
    top = jnp.floor(x * (1.0 / 65536.0))
    rest = x - top * modulus
    return jnp.where(rest >= modulus, rest - modulus, rest)


def digits(x):
    top = jnp.floor(x * (1.0 / 256.0))
    return top, x - top * 256.0


def stack_digits(x):
    top, low = digits(x)
    return jnp.concatenate([top, low], axis=0).astype(bf16)


def fold_two(top, low):
    return modp(modp(modp(top) * 256.0) + low)


def fold_three(upper, middle, lower):
    return modp(modp(upper) * 15.0 + modp(modp(middle) * 256.0) + lower)


def dot(a, b):
    return lax.dot_general(a, b, (((1,), (0,)), ((), ())), preferred_element_type=f32)


def dot_t(a, b):
    return lax.dot_general(a, b, (((1,), (1,)), ((), ())), preferred_element_type=f32)


def product(left, right):
    stacked = stack_digits(left)
    top, low = digits(right)
    by_top = dot(stacked, top.astype(bf16))
    by_low = dot(stacked, low.astype(bf16))
    return fold_three(by_top[:BLOCK], by_top[BLOCK:] + by_low[:BLOCK], by_low[BLOCK:])


def self_product(stacked):
    all_four = dot_t(stacked, stacked)
    by_top = all_four[:, :BLOCK]
    by_low = all_four[:, BLOCK:]
    return fold_three(by_top[:BLOCK], by_top[BLOCK:] + by_low[:BLOCK], by_low[BLOCK:])


def pack(matrix):
    return jnp.concatenate([matrix[8 * k : 8 * k + 8] for k in range(4)], axis=1)


def unpack(packed):
    return jnp.concatenate([packed[:, 32 * k : 32 * k + 32] for k in range(4)], axis=0)


def eye():
    rows = lax.broadcasted_iota(i32, (BLOCK, BLOCK), 0)
    cols = lax.broadcasted_iota(i32, (BLOCK, BLOCK), 1)
    return (rows == cols).astype(f32)


def shrink(x):
    return x - lax.shift_right_logical(x, 16) * PRIME


def settle(x):
    less = x - PRIME
    return jnp.where(less < 0, x, less)


def mulmod(a, b):
    return settle(shrink(shrink(a * b)))


def power(a):
    def fourth_up(x):
        for unused in range(4):
            x = mulmod(x, x)
        return x

    a2 = mulmod(a, a)
    a3 = mulmod(a2, a)
    a6 = mulmod(a3, a3)
    a12 = mulmod(a6, a6)
    a14 = mulmod(a12, a2)
    a15 = mulmod(a12, a3)
    a255 = mulmod(fourth_up(a15), a15)
    high = mulmod(fourth_up(a255), a14)
    return mulmod(fourth_up(high), a15)


def to_int(x):
    return x.astype(i32)


def lane_sum(x):
    return to_int(jnp.sum(x.astype(f32), axis=1, keepdims=True))


def sublane_sum(x):
    return to_int(jnp.sum(x.astype(f32), axis=0, keepdims=True))


def invert(gram, out_ref):
    wide = (BLOCK, 128)
    rows = lax.broadcasted_iota(i32, wide, 0)
    lanes = lax.broadcasted_iota(i32, wide, 1)
    start = jnp.concatenate([gram, eye(), jnp.zeros((BLOCK, 64), f32)], axis=1)
    start = to_int(start)

    def spread(row, column):
        return jnp.broadcast_to(matrix[row : row + 1, column : column + 1], wide)

    def small(x):
        return settle(shrink(x))

    shift = 17 * PRIME
    matrix = start
    least = jnp.full((1, 1), PRIME, i32)
    for c in range(0, BLOCK, 2):
        row_a = jnp.broadcast_to(matrix[c : c + 1, :], wide)
        row_b = jnp.broadcast_to(matrix[c + 1 : c + 2, :], wide)
        aa, ab, ba, bb = spread(c, c), spread(c, c + 1), spread(c + 1, c), spread(c + 1, c + 1)
        of_a = jnp.broadcast_to(matrix[:, c : c + 1], wide)
        of_b = jnp.broadcast_to(matrix[:, c + 1 : c + 2], wide)
        det = small(shrink(aa * bb) - shrink(ab * ba) + shift)
        least = jnp.minimum(least, jnp.minimum(aa[:1, :1], det[:1, :1]))
        new_a = small(shrink(bb * row_a) - shrink(ab * row_b) + shift)
        new_b = small(shrink(aa * row_b) - shrink(ba * row_a) + shift)
        updated = small(shrink(matrix * det) - shrink(of_a * new_a) - shrink(of_b * new_b) + 2 * shift)
        matrix = jnp.where(rows == c, new_a, jnp.where(rows == c + 1, new_b, updated))
    diagonal = lane_sum(jnp.where(rows == lanes, matrix, 0))
    scale = power(jnp.broadcast_to(diagonal, wide))
    out_ref[...] = mulmod(matrix, scale)[:, BLOCK : 2 * BLOCK].astype(f32)

    @pl.when(jnp.min(least.astype(f32)) == 0.0)
    def _():
        def eliminate(c, m):
            column = lane_sum(jnp.where(lanes == c, m, 0))
            row_ids = lax.broadcasted_iota(i32, (BLOCK, 1), 0)
            usable = (column != 0) & (row_ids >= c)
            at = jnp.min(jnp.where(usable, row_ids, BLOCK).astype(f32), axis=0, keepdims=True)
            at = to_int(at)
            at = jnp.where(at == BLOCK, c, at)
            at = jnp.broadcast_to(at, wide)
            pivot_row = jnp.broadcast_to(sublane_sum(jnp.where(rows == at, m, 0)), wide)
            current = jnp.broadcast_to(sublane_sum(jnp.where(rows == c, m, 0)), wide)
            swapped = jnp.where(rows == c, pivot_row, jnp.where(rows == at, current, m))
            pivot = jnp.broadcast_to(lane_sum(jnp.where(lanes == c, pivot_row, 0)), wide)
            scaled = mulmod(pivot_row, power(pivot))
            factors = jnp.broadcast_to(lane_sum(jnp.where(lanes == c, swapped, 0)), wide)
            reduced = settle(swapped - mulmod(factors, scaled) + PRIME)
            return jnp.where(rows == c, scaled, reduced)

        m = lax.fori_loop(0, BLOCK, eliminate, start)
        out_ref[...] = m[:, BLOCK : 2 * BLOCK].astype(f32)


def call(kernel, outs, args, smem=(), scratch=(), flops=0):
    specs = [
        pl.BlockSpec(memory_space=pltpu.SMEM if n in smem else pltpu.VMEM)
        for n in range(len(args))
    ]
    shapes = [jax.ShapeDtypeStruct(s, t) for s, t in outs]
    got = pl.pallas_call(
        kernel,
        out_shape=shapes,
        in_specs=specs,
        out_specs=[pl.BlockSpec(memory_space=pltpu.VMEM)] * len(shapes),
        scratch_shapes=list(scratch),
        compiler_params=pltpu.CompilerParams(vmem_limit_bytes=32 * 2**20),
        cost_estimate=pl.CostEstimate(flops=flops, bytes_accessed=4 * 2**20, transcendentals=0),
    )(*args)
    return got


def tile_at(t):
    return lax.rem(t, ROW_Y), lax.div(t, ROW_Y) * BLOCK


def forward(cols_ref, block_ref, tiles_ref, out_ref, count, slots):
    for r in range(count):
        total = None
        for s in range(slots):
            part, row = tile_at(cols_ref[r, s])
            picked = block_ref[part, pl.ds(pl.multiple_of(row, BLOCK), BLOCK), :]
            term = dot_t(stack_digits(picked), tiles_ref[r * slots + s])
            total = term if total is None else total + term
        out_ref[r * BLOCK : (r + 1) * BLOCK, :] = fold_two(total[:BLOCK], total[BLOCK:])


def backward(cols_ref, projected, tiles_ref, sums_ref, out_ref, count, slots):
    sums_ref[...] = jnp.zeros_like(sums_ref)
    gram = jnp.zeros((BLOCK, BLOCK), f32)
    for r in range(count):
        stacked = stack_digits(projected[r])
        gram = gram + self_product(stacked)
        for s in range(slots):
            t = cols_ref[r, s]
            sums_ref[t] += dot(stacked, tiles_ref[r * slots + s])
    for t in range(ROWS):
        whole = sums_ref[t]
        y, z = t % ROW_Y, t // ROW_Y
        out_ref[y, z * BLOCK : (z + 1) * BLOCK, :] = fold_two(whole[:BLOCK], whole[BLOCK:])
    packed = pack(modp(gram))
    for y in range(ROW_Y):
        out_ref[y, PART : PART + SMALL, :] = packed


def forward_first_kernel(count, slots, cols_ref, block_ref, entries_ref, out_ref, tiles_ref):
    for n in range(count * slots):
        tiles_ref[n] = entries_ref[n].astype(f32).astype(bf16)
    forward(cols_ref, block_ref, tiles_ref, out_ref, count, slots)


def forward_second_kernel(count, slots, cols_ref, block_ref, tiles_ref, out_ref):
    forward(cols_ref, block_ref, tiles_ref, out_ref, count, slots)
    square = block_ref[0, PART : PART + SMALL, :]
    for y in range(1, ROW_Y):
        square = square + block_ref[y, PART : PART + SMALL, :]
    out_ref[count * BLOCK : count * BLOCK + SMALL, :] = modp(square)


def backward_first_kernel(count, slots, cols_ref, own_ref, other_ref, tiles_ref, out_ref, y_ref, sums_ref):
    projected = []
    for r in range(count):
        at = slice(r * BLOCK, (r + 1) * BLOCK)
        value = modp(own_ref[at, :] + other_ref[at, :])
        y_ref[at, :] = value
        projected.append(value)
    backward(cols_ref, projected, tiles_ref, sums_ref, out_ref, count, slots)


def backward_second_kernel(
    count, slots, cols_ref, own_ref, other_ref, tiles_ref, gram_ref, inv_y_ref, inv_x_ref, old_ref, shifted_ref,
    out_ref, next_ref, result_ref, third_ref, sums_ref,
):
    small = slice(count * BLOCK, count * BLOCK + SMALL)
    square = unpack(modp(own_ref[small, :] + other_ref[small, :]))
    both = modp(square + gram_ref[...])
    projected = []
    for r in range(count):
        at = slice(r * BLOCK, (r + 1) * BLOCK)
        value = modp(own_ref[at, :] + other_ref[at, :])
        projected.append(modp(value - product(both, inv_y_ref[at, :]) + modulus))
    backward(cols_ref, projected, tiles_ref, sums_ref, out_ref, count, slots)
    following = modp(shifted_ref[...] - product(both, inv_x_ref[...]) + modulus)
    next_ref[...] = following
    result_ref[...] = following / modulus
    third_ref[...] = product(both, old_ref[...])


def sum_y_kernel(in_ref, out_ref):
    for z in range(ROW_Z):
        at = slice(z * BLOCK, (z + 1) * BLOCK)
        total = in_ref[0, at, :]
        for y in range(1, ROW_Y):
            total = total + in_ref[y, at, :]
        out_ref[z, :BLOCK, :] = total
    small = slice(PART, PART + SMALL)
    total = in_ref[0, small, :]
    for y in range(1, ROW_Y):
        total = total + in_ref[y, small, :]
    for z in range(ROW_Z):
        out_ref[z, BLOCK:, :] = total


def summed(in_ref):
    total = in_ref[0]
    for k in range(1, in_ref.shape[0]):
        total = total + in_ref[k]
    return modp(total)


def third_kernel(
    gram_ref, square_ref, inverse_ref, older_ref, now_ref, earlier_ref, earliest_ref, out_ref, float_inverse_ref, float_earlier_ref
):
    gram, inverse = gram_ref[...].astype(f32), inverse_ref[...].astype(f32)
    float_inverse_ref[...] = inverse
    float_earlier_ref[...] = earlier_ref[...].astype(f32)
    middle = modp(eye() - product(inverse, gram) + modulus)
    both = modp(square_ref[...].astype(f32) + gram)
    third = product(product(both, middle), older_ref[...].astype(f32))
    out_ref[...] = modp(now_ref[...] - product(third, earliest_ref[...].astype(f32)) + modulus)


def shift_kernel(in_ref, inverse_ref, earlier_ref, base_ref, out_ref, shifted_ref, gram_ref):
    total = summed(in_ref)
    applied = total[:BLOCK]
    gram = unpack(total[BLOCK:])
    gram_ref[...] = gram
    second = product(gram, inverse_ref[...])
    shifted = modp(applied + base_ref[...] + (modulus - product(second, earlier_ref[...])))
    shifted_ref[...] = shifted
    square = pack(self_product(stack_digits(applied)))
    for z in range(ROW_Z):
        out_ref[z, :BLOCK, :] = shifted
        out_ref[z, BLOCK:, :] = square


def spread_y_kernel(in_ref, out_ref):
    square = in_ref[0, BLOCK:, :]
    for z in range(1, ROW_Z):
        square = square + in_ref[z, BLOCK:, :]
    square = modp(square)
    for y in range(ROW_Y):
        for z in range(ROW_Z):
            out_ref[y, z * BLOCK : (z + 1) * BLOCK, :] = in_ref[z, :BLOCK, :]
        out_ref[y, PART:, :] = square


def inverse_kernel(
    count, gram_ref, older_ref, y_ref, now_ref, earlier_ref, inv_y_ref, inv_x_ref, old_ref, inverse_ref
):
    gram = gram_ref[...]
    invert(gram, inverse_ref)
    inverse = inverse_ref[...]
    for r in range(count):
        at = slice(r * BLOCK, (r + 1) * BLOCK)
        inv_y_ref[at, :] = product(inverse, y_ref[at, :])
    inv_x_ref[...] = product(inverse, now_ref[...])
    middle = modp(eye() - product(inverse, gram) + modulus)
    old_ref[...] = product(product(middle, older_ref[...]), earlier_ref[...])


def ending_kernel(in_ref, next_ref, inv_x_ref, third_ref, out_ref, base_ref, inv_next_ref, gram_ref, inverse_ref):
    total = summed(in_ref)
    applied = total[:BLOCK]
    gram = unpack(total[BLOCK:])
    gram_ref[...] = gram
    square = pack(self_product(stack_digits(applied)))
    for k in range(out_ref.shape[0]):
        out_ref[k] = square
    following = next_ref[...]
    minus = modp(product(gram, inv_x_ref[...]) + third_ref[...])
    base_ref[...] = modp(applied + following + (modulus - minus))
    invert(gram, inverse_ref)
    inv_next_ref[...] = product(inverse_ref[...], following)


def relay_kernel(in_ref, out_ref):
    total = summed(in_ref)
    for k in range(out_ref.shape[0]):
        out_ref[k] = total


def last_kernel(in_ref, gram_ref, base_ref, inv_next_ref, out_ref):
    both = modp(unpack(summed(in_ref)) + gram_ref[...])
    out_ref[...] = modp(base_ref[...] - product(both, inv_next_ref[...]) + modulus) / modulus


def exchange(parts, axis):
    return lax.all_to_all(parts, axis, 0, 0, tiled=True)


def flip(x, axis):
    return lax.ppermute(x, axis, [(0, 1), (1, 0)])


def together(*arrays):
    return lax.optimization_barrier(arrays)


def sum_core_x(partial):
    pair = partial + flip(partial, "c")
    return jnp.sum(exchange(jnp.broadcast_to(pair[None], (COL_X, *pair.shape)), "x"), axis=0)


def body(entries, tile_cols, block_now, block_prev, block_prev2, gram_prev, square_prev, inverse_prev, inverse_prev2):
    count, slots = tile_cols.shape
    length = count * BLOCK
    stored = entries.reshape(count * slots, TILE, TILE)
    current = block_now.astype(f32)
    shard = (BLOCK, TILE)
    small = (BLOCK, BLOCK)
    sums = [pltpu.VMEM((ROWS, 2 * BLOCK, TILE), f32)]

    along_z = exchange(jnp.broadcast_to(current[None], (ROW_Z, *shard)), "zl")
    block = exchange(jnp.broadcast_to(along_z.reshape(1, PART, TILE), (ROW_Y, PART, TILE)), "y")
    partial, tiles = call(
        functools.partial(forward_first_kernel, count, slots),
        [((length, TILE), f32), (stored.shape, bf16)], [tile_cols, block, stored], smem=(0,),
    )
    own = sum_core_x(partial)
    other = flip(own, "zh")
    own, *given = together(
        own, gram_prev, square_prev, inverse_prev, inverse_prev2, current, block_prev, block_prev2
    )
    base, inverse_old, earlier = call(
        third_kernel, [(shard, f32), (small, f32), (shard, f32)], given, flops=10**9
    )
    other, base, inverse_old, earlier = together(other, base, inverse_old, earlier)

    spread, projected = call(
        functools.partial(backward_first_kernel, count, slots),
        [((ROW_Y, PART + SMALL, TILE), f32), ((length, TILE), f32)],
        [tile_cols, own, other, tiles], smem=(0,), scratch=sums,
    )
    chunks = (ROW_Z, BLOCK + SMALL, TILE)
    [by_z] = call(sum_y_kernel, [(chunks, f32)], [exchange(spread, "y")])
    out, shifted, gram_now = call(
        shift_kernel, [(chunks, f32), (shard, f32), (small, f32)],
        [exchange(by_z, "zl"), inverse_old, earlier, base],
    )

    [spread] = call(spread_y_kernel, [((ROW_Y, PART + SMALL, TILE), f32)], [exchange(out, "zl")])
    [partial] = call(
        functools.partial(forward_second_kernel, count, slots),
        [((length + SMALL, TILE), f32)], [tile_cols, exchange(spread, "y"), tiles], smem=(0,),
    )
    own = sum_core_x(partial)
    other = flip(own, "zh")
    inv_y, inv_x, old, inverse_now = call(
        functools.partial(inverse_kernel, count),
        [((length, TILE), f32), (shard, f32), (shard, f32), (small, f32)],
        [gram_now, inverse_old, projected, current, earlier],
        flops=10**9,
    )
    spread, following, result, third = call(
        functools.partial(backward_second_kernel, count, slots),
        [((ROW_Y, PART + SMALL, TILE), f32), (shard, f32), (shard, f32), (shard, f32)],
        [tile_cols, own, other, tiles, gram_now, inv_y, inv_x, old, shifted], smem=(0,), scratch=sums,
    )
    [by_z] = call(sum_y_kernel, [(chunks, f32)], [exchange(spread, "y")])
    near = ROW_Y * COL_X * COL_C
    far = COL_Z * ROW_Z
    out, base, inv_next, gram_next, inverse_next = call(
        ending_kernel,
        [((far, SMALL, TILE), f32), (shard, f32), (shard, f32), (small, f32), (small, f32)],
        [exchange(by_z, "zl"), following, inv_x, third],
    )
    [out] = call(relay_kernel, [((near, SMALL, TILE), f32)], [exchange(out, ("zh", "zl"))])
    [later] = call(last_kernel, [(shard, f32)], [exchange(out, ("y", "x", "c")), gram_next, base, inv_next])
    return result, later


def solution(mesh):
    fine = Mesh(mesh.devices.reshape(ROW_Z, ROW_Y, COL_Z, COL_X, COL_C), ("zl", "y", "zh", "x", "c"))
    row, col = ("zl", "y"), ("zh", "x", "c")
    columns = P(None, (*col, *row))
    return jax.shard_map(
        body,
        mesh=fine,
        in_specs=(P(row, col, None, None), P(row, col), columns, columns, columns, P(), P(), P(), P()),
        out_specs=(columns, columns),
        check_vma=False,
    )
```

```python
import functools

import jax
import jax.numpy as jnp
from jax import lax
from jax.experimental import pallas as pl
from jax.experimental.pallas import tpu as pltpu
from jax.sharding import Mesh
from jax.sharding import PartitionSpec as P

PRIME = 65521
modulus = 65521.0
BLOCK = 32
TILE = 128
ROW_Z, ROW_Y = 8, 4
COL_Z, COL_X, COL_C = 2, 4, 2
ROWS = ROW_Z * ROW_Y
SMALL = 8
PART = ROW_Z * BLOCK

f32, bf16, i32 = jnp.float32, jnp.bfloat16, jnp.int32


def modp(x):
    top = jnp.floor(x * (1.0 / 65536.0))
    rest = x - top * modulus
    return jnp.where(rest >= modulus, rest - modulus, rest)


def digits(x):
    top = jnp.floor(x * (1.0 / 256.0))
    return top, x - top * 256.0


def stack_digits(x):
    top, low = digits(x)
    return jnp.concatenate([top, low], axis=0).astype(bf16)


def fold_two(top, low):
    return modp(modp(modp(top) * 256.0) + low)


def fold_three(upper, middle, lower):
    return modp(modp(upper) * 15.0 + modp(modp(middle) * 256.0) + lower)


def dot(a, b):
    return lax.dot_general(a, b, (((1,), (0,)), ((), ())), preferred_element_type=f32)


def dot_t(a, b):
    return lax.dot_general(a, b, (((1,), (1,)), ((), ())), preferred_element_type=f32)


def product(left, right):
    stacked = stack_digits(left)
    top, low = digits(right)
    by_top = dot(stacked, top.astype(bf16))
    by_low = dot(stacked, low.astype(bf16))
    return fold_three(by_top[:BLOCK], by_top[BLOCK:] + by_low[:BLOCK], by_low[BLOCK:])


def self_product(stacked):
    all_four = dot_t(stacked, stacked)
    by_top = all_four[:, :BLOCK]
    by_low = all_four[:, BLOCK:]
    return fold_three(by_top[:BLOCK], by_top[BLOCK:] + by_low[:BLOCK], by_low[BLOCK:])


def pack(matrix):
    return jnp.concatenate([matrix[8 * k : 8 * k + 8] for k in range(4)], axis=1)


def unpack(packed):
    return jnp.concatenate([packed[:, 32 * k : 32 * k + 32] for k in range(4)], axis=0)


def eye():
    rows = lax.broadcasted_iota(i32, (BLOCK, BLOCK), 0)
    cols = lax.broadcasted_iota(i32, (BLOCK, BLOCK), 1)
    return (rows == cols).astype(f32)


def shrink(x):
    return x - lax.shift_right_logical(x, 16) * PRIME


def settle(x):
    less = x - PRIME
    return jnp.where(less < 0, x, less)


def mulmod(a, b):
    return settle(shrink(shrink(a * b)))


def power(a):
    def fourth_up(x):
        for unused in range(4):
            x = mulmod(x, x)
        return x

    a2 = mulmod(a, a)
    a3 = mulmod(a2, a)
    a6 = mulmod(a3, a3)
    a12 = mulmod(a6, a6)
    a14 = mulmod(a12, a2)
    a15 = mulmod(a12, a3)
    a255 = mulmod(fourth_up(a15), a15)
    high = mulmod(fourth_up(a255), a14)
    return mulmod(fourth_up(high), a15)


def to_int(x):
    return x.astype(i32)


def lane_sum(x):
    return to_int(jnp.sum(x.astype(f32), axis=1, keepdims=True))


def sublane_sum(x):
    return to_int(jnp.sum(x.astype(f32), axis=0, keepdims=True))


def invert(gram, out_ref):
    wide = (BLOCK, 128)
    rows = lax.broadcasted_iota(i32, wide, 0)
    lanes = lax.broadcasted_iota(i32, wide, 1)
    start = jnp.concatenate([gram, eye(), jnp.zeros((BLOCK, 64), f32)], axis=1)
    start = to_int(start)

    def spread(row, column):
        return jnp.broadcast_to(matrix[row : row + 1, column : column + 1], wide)

    def small(x):
        return settle(shrink(x))

    shift = 17 * PRIME
    matrix = start
    least = jnp.full((1, 1), PRIME, i32)
    for c in range(0, BLOCK, 2):
        row_a = jnp.broadcast_to(matrix[c : c + 1, :], wide)
        row_b = jnp.broadcast_to(matrix[c + 1 : c + 2, :], wide)
        aa, ab, ba, bb = spread(c, c), spread(c, c + 1), spread(c + 1, c), spread(c + 1, c + 1)
        of_a = jnp.broadcast_to(matrix[:, c : c + 1], wide)
        of_b = jnp.broadcast_to(matrix[:, c + 1 : c + 2], wide)
        det = small(shrink(aa * bb) - shrink(ab * ba) + shift)
        least = jnp.minimum(least, jnp.minimum(aa[:1, :1], det[:1, :1]))
        new_a = small(shrink(bb * row_a) - shrink(ab * row_b) + shift)
        new_b = small(shrink(aa * row_b) - shrink(ba * row_a) + shift)
        updated = small(shrink(matrix * det) - shrink(of_a * new_a) - shrink(of_b * new_b) + 2 * shift)
        matrix = jnp.where(rows == c, new_a, jnp.where(rows == c + 1, new_b, updated))
    diagonal = lane_sum(jnp.where(rows == lanes, matrix, 0))
    scale = power(jnp.broadcast_to(diagonal, wide))
    out_ref[...] = mulmod(matrix, scale)[:, BLOCK : 2 * BLOCK].astype(f32)

    @pl.when(jnp.min(least.astype(f32)) == 0.0)
    def _():
        def eliminate(c, m):
            column = lane_sum(jnp.where(lanes == c, m, 0))
            row_ids = lax.broadcasted_iota(i32, (BLOCK, 1), 0)
            usable = (column != 0) & (row_ids >= c)
            at = jnp.min(jnp.where(usable, row_ids, BLOCK).astype(f32), axis=0, keepdims=True)
            at = to_int(at)
            at = jnp.where(at == BLOCK, c, at)
            at = jnp.broadcast_to(at, wide)
            pivot_row = jnp.broadcast_to(sublane_sum(jnp.where(rows == at, m, 0)), wide)
            current = jnp.broadcast_to(sublane_sum(jnp.where(rows == c, m, 0)), wide)
            swapped = jnp.where(rows == c, pivot_row, jnp.where(rows == at, current, m))
            pivot = jnp.broadcast_to(lane_sum(jnp.where(lanes == c, pivot_row, 0)), wide)
            scaled = mulmod(pivot_row, power(pivot))
            factors = jnp.broadcast_to(lane_sum(jnp.where(lanes == c, swapped, 0)), wide)
            reduced = settle(swapped - mulmod(factors, scaled) + PRIME)
            return jnp.where(rows == c, scaled, reduced)

        m = lax.fori_loop(0, BLOCK, eliminate, start)
        out_ref[...] = m[:, BLOCK : 2 * BLOCK].astype(f32)


def call(kernel, outs, args, smem=(), scratch=(), flops=0):
    specs = [
        pl.BlockSpec(memory_space=pltpu.SMEM if n in smem else pltpu.VMEM)
        for n in range(len(args))
    ]
    shapes = [jax.ShapeDtypeStruct(s, t) for s, t in outs]
    got = pl.pallas_call(
        kernel,
        out_shape=shapes,
        in_specs=specs,
        out_specs=[pl.BlockSpec(memory_space=pltpu.VMEM)] * len(shapes),
        scratch_shapes=list(scratch),
        compiler_params=pltpu.CompilerParams(vmem_limit_bytes=32 * 2**20),
        cost_estimate=pl.CostEstimate(flops=flops, bytes_accessed=4 * 2**20, transcendentals=0),
    )(*args)
    return got


def tile_at(t):
    return lax.rem(t, ROW_Y), lax.div(t, ROW_Y) * BLOCK


def forward(cols_ref, block_ref, tiles_ref, out_ref, count, slots):
    for r in range(count):
        total = None
        for s in range(slots):
            part, row = tile_at(cols_ref[r, s])
            picked = block_ref[part, pl.ds(pl.multiple_of(row, BLOCK), BLOCK), :]
            term = dot_t(stack_digits(picked), tiles_ref[r * slots + s])
            total = term if total is None else total + term
        out_ref[r * BLOCK : (r + 1) * BLOCK, :] = fold_two(total[:BLOCK], total[BLOCK:])


def backward(cols_ref, projected, tiles_ref, sums_ref, out_ref, count, slots):
    sums_ref[...] = jnp.zeros_like(sums_ref)
    gram = jnp.zeros((BLOCK, BLOCK), f32)
    for r in range(count):
        stacked = stack_digits(projected[r])
        gram = gram + self_product(stacked)
        for s in range(slots):
            t = cols_ref[r, s]
            sums_ref[t] += dot(stacked, tiles_ref[r * slots + s])
    for t in range(ROWS):
        whole = sums_ref[t]
        y, z = t % ROW_Y, t // ROW_Y
        out_ref[y, z * BLOCK : (z + 1) * BLOCK, :] = fold_two(whole[:BLOCK], whole[BLOCK:])
    packed = pack(modp(gram))
    for y in range(ROW_Y):
        out_ref[y, PART : PART + SMALL, :] = packed


def forward_first_kernel(count, slots, cols_ref, block_ref, entries_ref, out_ref, tiles_ref):
    for n in range(count * slots):
        tiles_ref[n] = entries_ref[n].astype(f32).astype(bf16)
    forward(cols_ref, block_ref, tiles_ref, out_ref, count, slots)


def forward_second_kernel(count, slots, cols_ref, block_ref, tiles_ref, out_ref):
    forward(cols_ref, block_ref, tiles_ref, out_ref, count, slots)
    square = block_ref[0, PART : PART + SMALL, :]
    for y in range(1, ROW_Y):
        square = square + block_ref[y, PART : PART + SMALL, :]
    out_ref[count * BLOCK : count * BLOCK + SMALL, :] = modp(square)


def backward_first_kernel(count, slots, cols_ref, own_ref, other_ref, tiles_ref, out_ref, y_ref, sums_ref):
    projected = []
    for r in range(count):
        at = slice(r * BLOCK, (r + 1) * BLOCK)
        value = modp(own_ref[at, :] + other_ref[at, :])
        y_ref[at, :] = value
        projected.append(value)
    backward(cols_ref, projected, tiles_ref, sums_ref, out_ref, count, slots)


def backward_second_kernel(
    count, slots, cols_ref, own_ref, other_ref, tiles_ref, gram_ref, inv_y_ref, out_ref, both_ref, sums_ref
):
    small = slice(count * BLOCK, count * BLOCK + SMALL)
    square = unpack(modp(own_ref[small, :] + other_ref[small, :]))
    both = modp(square + gram_ref[...])
    both_ref[...] = both
    projected = []
    for r in range(count):
        at = slice(r * BLOCK, (r + 1) * BLOCK)
        value = modp(own_ref[at, :] + other_ref[at, :])
        projected.append(modp(value - product(both, inv_y_ref[at, :]) + modulus))
    backward(cols_ref, projected, tiles_ref, sums_ref, out_ref, count, slots)


def sum_y_kernel(in_ref, out_ref):
    for z in range(ROW_Z):
        at = slice(z * BLOCK, (z + 1) * BLOCK)
        total = in_ref[0, at, :]
        for y in range(1, ROW_Y):
            total = total + in_ref[y, at, :]
        out_ref[z, :BLOCK, :] = total
    small = slice(PART, PART + SMALL)
    total = in_ref[0, small, :]
    for y in range(1, ROW_Y):
        total = total + in_ref[y, small, :]
    for z in range(ROW_Z):
        out_ref[z, BLOCK:, :] = total


def summed(in_ref):
    total = in_ref[0]
    for k in range(1, in_ref.shape[0]):
        total = total + in_ref[k]
    return modp(total)


def third_kernel(
    gram_ref, square_ref, inverse_ref, older_ref, now_ref, earlier_ref, earliest_ref, out_ref, float_inverse_ref, float_earlier_ref
):
    gram, inverse = gram_ref[...].astype(f32), inverse_ref[...].astype(f32)
    float_inverse_ref[...] = inverse
    float_earlier_ref[...] = earlier_ref[...].astype(f32)
    middle = modp(eye() - product(inverse, gram) + modulus)
    both = modp(square_ref[...].astype(f32) + gram)
    third = product(product(both, middle), older_ref[...].astype(f32))
    out_ref[...] = modp(now_ref[...] - product(third, earliest_ref[...].astype(f32)) + modulus)


def shift_kernel(in_ref, inverse_ref, earlier_ref, base_ref, out_ref, shifted_ref, gram_ref):
    total = summed(in_ref)
    applied = total[:BLOCK]
    gram = unpack(total[BLOCK:])
    gram_ref[...] = gram
    second = product(gram, inverse_ref[...])
    shifted = modp(applied + base_ref[...] + (modulus - product(second, earlier_ref[...])))
    shifted_ref[...] = shifted
    square = pack(self_product(stack_digits(applied)))
    for z in range(ROW_Z):
        out_ref[z, :BLOCK, :] = shifted
        out_ref[z, BLOCK:, :] = square


def spread_y_kernel(in_ref, out_ref):
    square = in_ref[0, BLOCK:, :]
    for z in range(1, ROW_Z):
        square = square + in_ref[z, BLOCK:, :]
    square = modp(square)
    for y in range(ROW_Y):
        for z in range(ROW_Z):
            out_ref[y, z * BLOCK : (z + 1) * BLOCK, :] = in_ref[z, :BLOCK, :]
        out_ref[y, PART:, :] = square


def inverse_kernel(
    count, gram_ref, older_ref, y_ref, now_ref, earlier_ref, inv_y_ref, inv_x_ref, old_ref, inverse_ref
):
    gram = gram_ref[...]
    invert(gram, inverse_ref)
    inverse = inverse_ref[...]
    for r in range(count):
        at = slice(r * BLOCK, (r + 1) * BLOCK)
        inv_y_ref[at, :] = product(inverse, y_ref[at, :])
    inv_x_ref[...] = product(inverse, now_ref[...])
    middle = modp(eye() - product(inverse, gram) + modulus)
    old_ref[...] = product(product(middle, older_ref[...]), earlier_ref[...])


def ending_kernel(
    in_ref, both_ref, shifted_ref, inv_x_ref, old_ref, out_ref, result_ref, base_ref, gram_ref, inverse_ref, inv_next_ref
):
    total = summed(in_ref)
    applied = total[:BLOCK]
    gram = unpack(total[BLOCK:])
    gram_ref[...] = gram
    square = pack(self_product(stack_digits(applied)))
    for k in range(out_ref.shape[0]):
        out_ref[k] = square
    both = both_ref[...]
    following = modp(shifted_ref[...] - product(both, inv_x_ref[...]) + modulus)
    result_ref[...] = following / modulus
    minus = modp(product(gram, inv_x_ref[...]) + product(both, old_ref[...]))
    base_ref[...] = modp(applied + following + (modulus - minus))
    invert(gram, inverse_ref)
    inv_next_ref[...] = product(inverse_ref[...], following)


def relay_kernel(in_ref, out_ref):
    total = summed(in_ref)
    for k in range(out_ref.shape[0]):
        out_ref[k] = total


def last_kernel(in_ref, gram_ref, base_ref, inv_next_ref, out_ref):
    both = modp(unpack(summed(in_ref)) + gram_ref[...])
    out_ref[...] = modp(base_ref[...] - product(both, inv_next_ref[...]) + modulus) / modulus


def exchange(parts, axis):
    return lax.all_to_all(parts, axis, 0, 0, tiled=True)


def flip(x, axis):
    return lax.ppermute(x, axis, [(0, 1), (1, 0)])


def together(*arrays):
    return lax.optimization_barrier(arrays)


def sum_core_x(partial):
    pair = partial + flip(partial, "c")
    return jnp.sum(exchange(jnp.broadcast_to(pair[None], (COL_X, *pair.shape)), "x"), axis=0)


def body(entries, tile_cols, block_now, block_prev, block_prev2, gram_prev, square_prev, inverse_prev, inverse_prev2):
    count, slots = tile_cols.shape
    length = count * BLOCK
    stored = entries.reshape(count * slots, TILE, TILE)
    current = block_now.astype(f32)
    shard = (BLOCK, TILE)
    small = (BLOCK, BLOCK)
    sums = [pltpu.VMEM((ROWS, 2 * BLOCK, TILE), f32)]

    along_z = exchange(jnp.broadcast_to(current[None], (ROW_Z, *shard)), "zl")
    block = exchange(jnp.broadcast_to(along_z.reshape(1, PART, TILE), (ROW_Y, PART, TILE)), "y")
    partial, tiles = call(
        functools.partial(forward_first_kernel, count, slots),
        [((length, TILE), f32), (stored.shape, bf16)], [tile_cols, block, stored], smem=(0,),
    )
    own = sum_core_x(partial)
    other = flip(own, "zh")
    own, *given = together(
        own, gram_prev, square_prev, inverse_prev, inverse_prev2, current, block_prev, block_prev2
    )
    base, inverse_old, earlier = call(
        third_kernel, [(shard, f32), (small, f32), (shard, f32)], given, flops=10**9
    )
    other, base, inverse_old, earlier = together(other, base, inverse_old, earlier)

    spread, projected = call(
        functools.partial(backward_first_kernel, count, slots),
        [((ROW_Y, PART + SMALL, TILE), f32), ((length, TILE), f32)],
        [tile_cols, own, other, tiles], smem=(0,), scratch=sums,
    )
    chunks = (ROW_Z, BLOCK + SMALL, TILE)
    [by_z] = call(sum_y_kernel, [(chunks, f32)], [exchange(spread, "y")])
    out, shifted, gram_now = call(
        shift_kernel, [(chunks, f32), (shard, f32), (small, f32)],
        [exchange(by_z, "zl"), inverse_old, earlier, base],
    )

    [spread] = call(spread_y_kernel, [((ROW_Y, PART + SMALL, TILE), f32)], [exchange(out, "zl")])
    [partial] = call(
        functools.partial(forward_second_kernel, count, slots),
        [((length + SMALL, TILE), f32)], [tile_cols, exchange(spread, "y"), tiles], smem=(0,),
    )
    own = sum_core_x(partial)
    other = flip(own, "zh")
    inv_y, inv_x, old, inverse_now = call(
        functools.partial(inverse_kernel, count),
        [((length, TILE), f32), (shard, f32), (shard, f32), (small, f32)],
        [gram_now, inverse_old, projected, current, earlier],
        flops=10**9,
    )
    spread, both = call(
        functools.partial(backward_second_kernel, count, slots),
        [((ROW_Y, PART + SMALL, TILE), f32), (small, f32)],
        [tile_cols, own, other, tiles, gram_now, inv_y], smem=(0,), scratch=sums,
    )
    [by_z] = call(sum_y_kernel, [(chunks, f32)], [exchange(spread, "y")])
    near = ROW_Y * COL_X * COL_C
    far = COL_Z * ROW_Z
    out, result, base, gram_next, inverse_next, inv_next = call(
        ending_kernel,
        [((near, SMALL, TILE), f32), (shard, f32), (shard, f32), (small, f32), (small, f32), (shard, f32)],
        [exchange(by_z, "zl"), both, shifted, inv_x, old],
    )
    [out] = call(relay_kernel, [((far, SMALL, TILE), f32)], [exchange(out, ("y", "x", "c"))])
    [later] = call(last_kernel, [(shard, f32)], [exchange(out, ("zh", "zl")), gram_next, base, inv_next])
    return result, later


def solution(mesh):
    fine = Mesh(mesh.devices.reshape(ROW_Z, ROW_Y, COL_Z, COL_X, COL_C), ("zl", "y", "zh", "x", "c"))
    row, col = ("zl", "y"), ("zh", "x", "c")
    columns = P(None, (*col, *row))
    return jax.shard_map(
        body,
        mesh=fine,
        in_specs=(P(row, col, None, None), P(row, col), columns, columns, columns, P(), P(), P(), P()),
        out_specs=(columns, columns),
        check_vma=False,
    )
```

```python
import functools

import jax
import jax.numpy as jnp
from jax import lax
from jax.experimental import pallas as pl
from jax.experimental.pallas import tpu as pltpu
from jax.sharding import Mesh
from jax.sharding import PartitionSpec as P

PRIME = 65521
modulus = 65521.0
BLOCK = 32
TILE = 128
ROW_Z, ROW_Y = 8, 4
COL_Z, COL_X, COL_C = 2, 4, 2
ROWS = ROW_Z * ROW_Y
AHEAD = 3
SMALL = 8
PART = ROW_Z * BLOCK

f32, bf16, i32 = jnp.float32, jnp.bfloat16, jnp.int32


def modp(x):
    top = jnp.floor(x * (1.0 / 65536.0))
    rest = x - top * modulus
    return jnp.where(rest >= modulus, rest - modulus, rest)


def digits(x):
    top = jnp.floor(x * (1.0 / 256.0))
    return top, x - top * 256.0


def stack_digits(x):
    top, low = digits(x)
    return jnp.concatenate([top, low], axis=0).astype(bf16)


def fold_two(top, low):
    return modp(modp(modp(top) * 256.0) + low)


def fold_three(upper, middle, lower):
    return modp(modp(upper) * 15.0 + modp(modp(middle) * 256.0) + lower)


def dot(a, b):
    return lax.dot_general(a, b, (((1,), (0,)), ((), ())), preferred_element_type=f32)


def dot_t(a, b):
    return lax.dot_general(a, b, (((1,), (1,)), ((), ())), preferred_element_type=f32)


def product(left, right):
    stacked = stack_digits(left)
    top, low = digits(right)
    by_top = dot(stacked, top.astype(bf16))
    by_low = dot(stacked, low.astype(bf16))
    return fold_three(by_top[:BLOCK], by_top[BLOCK:] + by_low[:BLOCK], by_low[BLOCK:])


def self_product(stacked):
    all_four = dot_t(stacked, stacked)
    by_top = all_four[:, :BLOCK]
    by_low = all_four[:, BLOCK:]
    return fold_three(by_top[:BLOCK], by_top[BLOCK:] + by_low[:BLOCK], by_low[BLOCK:])


def pack(matrix):
    return jnp.concatenate([matrix[8 * k : 8 * k + 8] for k in range(4)], axis=1)


def unpack(packed):
    return jnp.concatenate([packed[:, 32 * k : 32 * k + 32] for k in range(4)], axis=0)


def eye():
    rows = lax.broadcasted_iota(i32, (BLOCK, BLOCK), 0)
    cols = lax.broadcasted_iota(i32, (BLOCK, BLOCK), 1)
    return (rows == cols).astype(f32)


def shrink(x):
    return x - lax.shift_right_logical(x, 16) * PRIME


def settle(x):
    less = x - PRIME
    return jnp.where(less < 0, x, less)


def mulmod(a, b):
    return settle(shrink(shrink(a * b)))


def power(a):
    def fourth_up(x):
        for unused in range(4):
            x = mulmod(x, x)
        return x

    a2 = mulmod(a, a)
    a3 = mulmod(a2, a)
    a6 = mulmod(a3, a3)
    a12 = mulmod(a6, a6)
    a14 = mulmod(a12, a2)
    a15 = mulmod(a12, a3)
    a255 = mulmod(fourth_up(a15), a15)
    high = mulmod(fourth_up(a255), a14)
    return mulmod(fourth_up(high), a15)


def to_int(x):
    return x.astype(i32)


def lane_sum(x):
    return to_int(jnp.sum(x.astype(f32), axis=1, keepdims=True))


def sublane_sum(x):
    return to_int(jnp.sum(x.astype(f32), axis=0, keepdims=True))


def invert(gram, out_ref):
    wide = (BLOCK, 128)
    rows = lax.broadcasted_iota(i32, wide, 0)
    lanes = lax.broadcasted_iota(i32, wide, 1)
    start = jnp.concatenate([gram, eye(), jnp.zeros((BLOCK, 64), f32)], axis=1)
    start = to_int(start)

    def four(x):
        return jnp.concatenate([x] * 4, axis=0)

    def row_of(x, c):
        return jnp.broadcast_to(x[c : c + 1], (8, 128))

    def column_of(x, c):
        return jnp.broadcast_to(x[:, c : c + 1], wide)

    matrix = start
    least = jnp.full((1, 1), PRIME, i32)
    fetched = [column_of(matrix, c) for c in range(AHEAD)]
    for c in range(BLOCK):
        factors = fetched[0]
        pivot = row_of(factors, c)
        least = jnp.minimum(least, pivot[:1, :1])

        def step(x):
            kept = shrink(x * four(pivot))
            taken = shrink(factors * four(row_of(x, c)))
            return jnp.where(rows == c, x, settle(shrink(kept - taken + 17 * PRIME)))

        waiting = fetched[1:]
        if c + AHEAD < BLOCK:
            waiting.append(column_of(matrix, c + AHEAD))
        fetched = [step(x) for x in waiting]
        matrix = step(matrix)
    diagonal = lane_sum(jnp.where(rows == lanes, matrix, 0))
    scale = power(jnp.broadcast_to(diagonal, wide))
    out_ref[...] = mulmod(matrix, scale)[:, BLOCK : 2 * BLOCK].astype(f32)

    @pl.when(jnp.min(least.astype(f32)) == 0.0)
    def _():
        def eliminate(c, m):
            column = lane_sum(jnp.where(lanes == c, m, 0))
            row_ids = lax.broadcasted_iota(i32, (BLOCK, 1), 0)
            usable = (column != 0) & (row_ids >= c)
            at = jnp.min(jnp.where(usable, row_ids, BLOCK).astype(f32), axis=0, keepdims=True)
            at = to_int(at)
            at = jnp.where(at == BLOCK, c, at)
            at = jnp.broadcast_to(at, wide)
            pivot_row = jnp.broadcast_to(sublane_sum(jnp.where(rows == at, m, 0)), wide)
            current = jnp.broadcast_to(sublane_sum(jnp.where(rows == c, m, 0)), wide)
            swapped = jnp.where(rows == c, pivot_row, jnp.where(rows == at, current, m))
            pivot = jnp.broadcast_to(lane_sum(jnp.where(lanes == c, pivot_row, 0)), wide)
            scaled = mulmod(pivot_row, power(pivot))
            factors = jnp.broadcast_to(lane_sum(jnp.where(lanes == c, swapped, 0)), wide)
            reduced = settle(swapped - mulmod(factors, scaled) + PRIME)
            return jnp.where(rows == c, scaled, reduced)

        m = lax.fori_loop(0, BLOCK, eliminate, start)
        out_ref[...] = m[:, BLOCK : 2 * BLOCK].astype(f32)


def call(kernel, outs, args, smem=(), scratch=(), flops=0):
    specs = [
        pl.BlockSpec(memory_space=pltpu.SMEM if n in smem else pltpu.VMEM)
        for n in range(len(args))
    ]
    shapes = [jax.ShapeDtypeStruct(s, t) for s, t in outs]
    got = pl.pallas_call(
        kernel,
        out_shape=shapes,
        in_specs=specs,
        out_specs=[pl.BlockSpec(memory_space=pltpu.VMEM)] * len(shapes),
        scratch_shapes=list(scratch),
        compiler_params=pltpu.CompilerParams(vmem_limit_bytes=32 * 2**20),
        cost_estimate=pl.CostEstimate(flops=flops, bytes_accessed=4 * 2**20, transcendentals=0),
    )(*args)
    return got


def tile_at(t):
    return lax.rem(t, ROW_Y), lax.div(t, ROW_Y) * BLOCK


def forward(cols_ref, block_ref, tiles_ref, out_ref, count, slots):
    for r in range(count):
        total = None
        for s in range(0, slots, 2):
            pair = []
            for k in (s, s + 1):
                part, row = tile_at(cols_ref[r, k])
                pair.append(stack_digits(block_ref[part, pl.ds(pl.multiple_of(row, BLOCK), BLOCK), :]))
            at = r * slots + s
            stored = jnp.concatenate([tiles_ref[at], tiles_ref[at + 1]], axis=1)
            term = dot_t(jnp.concatenate(pair, axis=1), stored)
            total = term if total is None else total + term
        out_ref[r * BLOCK : (r + 1) * BLOCK, :] = fold_two(total[:BLOCK], total[BLOCK:])


def backward(cols_ref, projected, tiles_ref, sums_ref, out_ref, count, slots):
    sums_ref[...] = jnp.zeros_like(sums_ref)
    gram = jnp.zeros((BLOCK, BLOCK), f32)
    for r in range(count):
        stacked = stack_digits(projected[r])
        gram = gram + self_product(stacked)
        for s in range(0, slots, 2):
            at = r * slots + s
            terms = dot(stacked, jnp.concatenate([tiles_ref[at], tiles_ref[at + 1]], axis=1))
            sums_ref[cols_ref[r, s]] += terms[:, :TILE]
            sums_ref[cols_ref[r, s + 1]] += terms[:, TILE:]
    for t in range(ROWS):
        whole = sums_ref[t]
        y, z = t % ROW_Y, t // ROW_Y
        out_ref[y, z * BLOCK : (z + 1) * BLOCK, :] = fold_two(whole[:BLOCK], whole[BLOCK:])
    packed = pack(modp(gram))
    for y in range(ROW_Y):
        out_ref[y, PART : PART + SMALL, :] = packed


def forward_first_kernel(count, slots, cols_ref, block_ref, entries_ref, out_ref, tiles_ref):
    for n in range(count * slots):
        tiles_ref[n] = entries_ref[n].astype(f32).astype(bf16)
    forward(cols_ref, block_ref, tiles_ref, out_ref, count, slots)


def forward_second_kernel(count, slots, cols_ref, block_ref, tiles_ref, out_ref):
    forward(cols_ref, block_ref, tiles_ref, out_ref, count, slots)
    square = block_ref[0, PART : PART + SMALL, :]
    for y in range(1, ROW_Y):
        square = square + block_ref[y, PART : PART + SMALL, :]
    out_ref[count * BLOCK : count * BLOCK + SMALL, :] = modp(square)


def backward_first_kernel(count, slots, cols_ref, own_ref, other_ref, tiles_ref, out_ref, y_ref, sums_ref):
    projected = []
    for r in range(count):
        at = slice(r * BLOCK, (r + 1) * BLOCK)
        value = modp(own_ref[at, :] + other_ref[at, :])
        y_ref[at, :] = value
        projected.append(value)
    backward(cols_ref, projected, tiles_ref, sums_ref, out_ref, count, slots)


def backward_second_kernel(
    count, slots, cols_ref, own_ref, other_ref, tiles_ref, gram_ref, inv_y_ref, out_ref, both_ref, sums_ref
):
    small = slice(count * BLOCK, count * BLOCK + SMALL)
    square = unpack(modp(own_ref[small, :] + other_ref[small, :]))
    both = modp(square + gram_ref[...])
    both_ref[...] = both
    projected = []
    for r in range(count):
        at = slice(r * BLOCK, (r + 1) * BLOCK)
        value = modp(own_ref[at, :] + other_ref[at, :])
        projected.append(modp(value - product(both, inv_y_ref[at, :]) + modulus))
    backward(cols_ref, projected, tiles_ref, sums_ref, out_ref, count, slots)


def sum_y_kernel(in_ref, out_ref):
    for z in range(ROW_Z):
        at = slice(z * BLOCK, (z + 1) * BLOCK)
        total = in_ref[0, at, :]
        for y in range(1, ROW_Y):
            total = total + in_ref[y, at, :]
        out_ref[z, :BLOCK, :] = total
    small = slice(PART, PART + SMALL)
    total = in_ref[0, small, :]
    for y in range(1, ROW_Y):
        total = total + in_ref[y, small, :]
    for z in range(ROW_Z):
        out_ref[z, BLOCK:, :] = total


def summed(in_ref):
    total = in_ref[0]
    for k in range(1, in_ref.shape[0]):
        total = total + in_ref[k]
    return modp(total)


def third_kernel(
    gram_ref, square_ref, inverse_ref, older_ref, now_ref, earlier_ref, earliest_ref, out_ref, float_inverse_ref, float_earlier_ref
):
    gram, inverse = gram_ref[...].astype(f32), inverse_ref[...].astype(f32)
    float_inverse_ref[...] = inverse
    float_earlier_ref[...] = earlier_ref[...].astype(f32)
    middle = modp(eye() - product(inverse, gram) + modulus)
    both = modp(square_ref[...].astype(f32) + gram)
    third = product(product(both, middle), older_ref[...].astype(f32))
    out_ref[...] = modp(now_ref[...] - product(third, earliest_ref[...].astype(f32)) + modulus)


def shift_kernel(in_ref, inverse_ref, earlier_ref, base_ref, out_ref, shifted_ref, gram_ref):
    total = summed(in_ref)
    applied = total[:BLOCK]
    gram = unpack(total[BLOCK:])
    gram_ref[...] = gram
    second = product(gram, inverse_ref[...])
    shifted = modp(applied + base_ref[...] + (modulus - product(second, earlier_ref[...])))
    shifted_ref[...] = shifted
    square = pack(self_product(stack_digits(applied)))
    for z in range(ROW_Z):
        out_ref[z, :BLOCK, :] = shifted
        out_ref[z, BLOCK:, :] = square


def spread_y_kernel(in_ref, out_ref):
    square = in_ref[0, BLOCK:, :]
    for z in range(1, ROW_Z):
        square = square + in_ref[z, BLOCK:, :]
    square = modp(square)
    for y in range(ROW_Y):
        for z in range(ROW_Z):
            out_ref[y, z * BLOCK : (z + 1) * BLOCK, :] = in_ref[z, :BLOCK, :]
        out_ref[y, PART:, :] = square


def inverse_kernel(
    count, gram_ref, older_ref, y_ref, now_ref, earlier_ref, inv_y_ref, inv_x_ref, old_ref, inverse_ref
):
    gram = gram_ref[...]
    invert(gram, inverse_ref)
    inverse = inverse_ref[...]
    for r in range(count):
        at = slice(r * BLOCK, (r + 1) * BLOCK)
        inv_y_ref[at, :] = product(inverse, y_ref[at, :])
    inv_x_ref[...] = product(inverse, now_ref[...])
    middle = modp(eye() - product(inverse, gram) + modulus)
    old_ref[...] = product(product(middle, older_ref[...]), earlier_ref[...])


def ending_kernel(
    in_ref, both_ref, shifted_ref, inv_x_ref, old_ref, out_ref, result_ref, base_ref, gram_ref, inverse_ref, inv_next_ref
):
    total = summed(in_ref)
    applied = total[:BLOCK]
    gram = unpack(total[BLOCK:])
    gram_ref[...] = gram
    square = pack(self_product(stack_digits(applied)))
    for k in range(out_ref.shape[0]):
        out_ref[k] = square
    both = both_ref[...]
    following = modp(shifted_ref[...] - product(both, inv_x_ref[...]) + modulus)
    result_ref[...] = following / modulus
    minus = modp(product(gram, inv_x_ref[...]) + product(both, old_ref[...]))
    base_ref[...] = modp(applied + following + (modulus - minus))
    invert(gram, inverse_ref)
    inv_next_ref[...] = product(inverse_ref[...], following)


def relay_kernel(in_ref, out_ref):
    total = summed(in_ref)
    for k in range(out_ref.shape[0]):
        out_ref[k] = total


def last_kernel(in_ref, gram_ref, base_ref, inv_next_ref, out_ref):
    both = modp(unpack(summed(in_ref)) + gram_ref[...])
    out_ref[...] = modp(base_ref[...] - product(both, inv_next_ref[...]) + modulus) / modulus


def exchange(parts, axis):
    return lax.all_to_all(parts, axis, 0, 0, tiled=True)


def flip(x, axis):
    return lax.ppermute(x, axis, [(0, 1), (1, 0)])


def together(*arrays):
    return lax.optimization_barrier(arrays)


def sum_core_x(partial):
    pair = partial + flip(partial, "c")
    return jnp.sum(exchange(jnp.broadcast_to(pair[None], (COL_X, *pair.shape)), "x"), axis=0)


def body(entries, tile_cols, block_now, block_prev, block_prev2, gram_prev, square_prev, inverse_prev, inverse_prev2):
    count, slots = tile_cols.shape
    length = count * BLOCK
    stored = entries.reshape(count * slots, TILE, TILE)
    current = block_now.astype(f32)
    shard = (BLOCK, TILE)
    small = (BLOCK, BLOCK)
    sums = [pltpu.VMEM((ROWS, 2 * BLOCK, TILE), f32)]

    along_z = exchange(jnp.broadcast_to(current[None], (ROW_Z, *shard)), "zl")
    block = exchange(jnp.broadcast_to(along_z.reshape(1, PART, TILE), (ROW_Y, PART, TILE)), "y")
    partial, tiles = call(
        functools.partial(forward_first_kernel, count, slots),
        [((length, TILE), f32), (stored.shape, bf16)], [tile_cols, block, stored], smem=(0,),
    )
    own = sum_core_x(partial)
    other = flip(own, "zh")
    own, *given = together(
        own, gram_prev, square_prev, inverse_prev, inverse_prev2, current, block_prev, block_prev2
    )
    base, inverse_old, earlier = call(
        third_kernel, [(shard, f32), (small, f32), (shard, f32)], given, flops=10**9
    )
    other, base, inverse_old, earlier = together(other, base, inverse_old, earlier)

    spread, projected = call(
        functools.partial(backward_first_kernel, count, slots),
        [((ROW_Y, PART + SMALL, TILE), f32), ((length, TILE), f32)],
        [tile_cols, own, other, tiles], smem=(0,), scratch=sums,
    )
    chunks = (ROW_Z, BLOCK + SMALL, TILE)
    [by_z] = call(sum_y_kernel, [(chunks, f32)], [exchange(spread, "y")])
    out, shifted, gram_now = call(
        shift_kernel, [(chunks, f32), (shard, f32), (small, f32)],
        [exchange(by_z, "zl"), inverse_old, earlier, base],
    )

    [spread] = call(spread_y_kernel, [((ROW_Y, PART + SMALL, TILE), f32)], [exchange(out, "zl")])
    [partial] = call(
        functools.partial(forward_second_kernel, count, slots),
        [((length + SMALL, TILE), f32)], [tile_cols, exchange(spread, "y"), tiles], smem=(0,),
    )
    own = sum_core_x(partial)
    other = flip(own, "zh")
    inv_y, inv_x, old, inverse_now = call(
        functools.partial(inverse_kernel, count),
        [((length, TILE), f32), (shard, f32), (shard, f32), (small, f32)],
        [gram_now, inverse_old, projected, current, earlier],
        flops=10**9,
    )
    spread, both = call(
        functools.partial(backward_second_kernel, count, slots),
        [((ROW_Y, PART + SMALL, TILE), f32), (small, f32)],
        [tile_cols, own, other, tiles, gram_now, inv_y], smem=(0,), scratch=sums,
    )
    [by_z] = call(sum_y_kernel, [(chunks, f32)], [exchange(spread, "y")])
    near = ROW_Y * COL_X * COL_C
    far = COL_Z * ROW_Z
    out, result, base, gram_next, inverse_next, inv_next = call(
        ending_kernel,
        [((near, SMALL, TILE), f32), (shard, f32), (shard, f32), (small, f32), (small, f32), (shard, f32)],
        [exchange(by_z, "zl"), both, shifted, inv_x, old],
    )
    [out] = call(relay_kernel, [((far, SMALL, TILE), f32)], [exchange(out, ("y", "x", "c"))])
    [later] = call(last_kernel, [(shard, f32)], [exchange(out, ("zh", "zl")), gram_next, base, inv_next])
    return result, later


def solution(mesh):
    fine = Mesh(mesh.devices.reshape(ROW_Z, ROW_Y, COL_Z, COL_X, COL_C), ("zl", "y", "zh", "x", "c"))
    row, col = ("zl", "y"), ("zh", "x", "c")
    columns = P(None, (*col, *row))
    return jax.shard_map(
        body,
        mesh=fine,
        in_specs=(P(row, col, None, None), P(row, col), columns, columns, columns, P(), P(), P(), P()),
        out_specs=(columns, columns),
        check_vma=False,
    )
```

```python
import functools

import jax
import jax.numpy as jnp
from jax import lax
from jax.experimental import pallas as pl
from jax.experimental.pallas import tpu as pltpu
from jax.sharding import Mesh
from jax.sharding import PartitionSpec as P

PRIME = 65521
modulus = 65521.0
BLOCK = 32
TILE = 128
ROW_Z, ROW_Y = 8, 4
COL_Z, COL_X, COL_C = 2, 4, 2
Z_LO = ("z0", "z2", "z1")
ROWS = ROW_Z * ROW_Y
AHEAD = 3
SMALL = 8
PART = ROW_Z * BLOCK

f32, bf16, i32 = jnp.float32, jnp.bfloat16, jnp.int32


def modp(x):
    top = jnp.floor(x * (1.0 / 65536.0))
    rest = x - top * modulus
    return jnp.where(rest >= modulus, rest - modulus, rest)


def digits(x):
    top = jnp.floor(x * (1.0 / 256.0))
    return top, x - top * 256.0


def stack_digits(x):
    top, low = digits(x)
    return jnp.concatenate([top, low], axis=0).astype(bf16)


def fold_two(top, low):
    return modp(modp(modp(top) * 256.0) + low)


def fold_three(upper, middle, lower):
    return modp(modp(upper) * 15.0 + modp(modp(middle) * 256.0) + lower)


def dot(a, b):
    return lax.dot_general(a, b, (((1,), (0,)), ((), ())), preferred_element_type=f32)


def dot_t(a, b):
    return lax.dot_general(a, b, (((1,), (1,)), ((), ())), preferred_element_type=f32)


def product(left, right):
    stacked = stack_digits(left)
    top, low = digits(right)
    by_top = dot(stacked, top.astype(bf16))
    by_low = dot(stacked, low.astype(bf16))
    return fold_three(by_top[:BLOCK], by_top[BLOCK:] + by_low[:BLOCK], by_low[BLOCK:])


def self_product(stacked):
    all_four = dot_t(stacked, stacked)
    by_top = all_four[:, :BLOCK]
    by_low = all_four[:, BLOCK:]
    return fold_three(by_top[:BLOCK], by_top[BLOCK:] + by_low[:BLOCK], by_low[BLOCK:])


def pack(matrix):
    return jnp.concatenate([matrix[8 * k : 8 * k + 8] for k in range(4)], axis=1)


def unpack(packed):
    return jnp.concatenate([packed[:, 32 * k : 32 * k + 32] for k in range(4)], axis=0)


def eye():
    rows = lax.broadcasted_iota(i32, (BLOCK, BLOCK), 0)
    cols = lax.broadcasted_iota(i32, (BLOCK, BLOCK), 1)
    return (rows == cols).astype(f32)


def shrink(x):
    return x - lax.shift_right_logical(x, 16) * PRIME


def settle(x):
    less = x - PRIME
    return jnp.where(less < 0, x, less)


def mulmod(a, b):
    return settle(shrink(shrink(a * b)))


def power(a):
    def fourth_up(x):
        for unused in range(4):
            x = mulmod(x, x)
        return x

    a2 = mulmod(a, a)
    a3 = mulmod(a2, a)
    a6 = mulmod(a3, a3)
    a12 = mulmod(a6, a6)
    a14 = mulmod(a12, a2)
    a15 = mulmod(a12, a3)
    a255 = mulmod(fourth_up(a15), a15)
    high = mulmod(fourth_up(a255), a14)
    return mulmod(fourth_up(high), a15)


def to_int(x):
    return x.astype(i32)


def lane_sum(x):
    return to_int(jnp.sum(x.astype(f32), axis=1, keepdims=True))


def sublane_sum(x):
    return to_int(jnp.sum(x.astype(f32), axis=0, keepdims=True))


def invert(gram, out_ref):
    wide = (BLOCK, 128)
    rows = lax.broadcasted_iota(i32, wide, 0)
    lanes = lax.broadcasted_iota(i32, wide, 1)
    start = jnp.concatenate([gram, eye(), jnp.zeros((BLOCK, 64), f32)], axis=1)
    start = to_int(start)

    def four(x):
        return jnp.concatenate([x] * 4, axis=0)

    def row_of(x, c):
        return jnp.broadcast_to(x[c : c + 1], (8, 128))

    def column_of(x, c):
        return jnp.broadcast_to(x[:, c : c + 1], wide)

    matrix = start
    least = jnp.full((1, 1), PRIME, i32)
    fetched = [column_of(matrix, c) for c in range(AHEAD)]
    for c in range(BLOCK):
        factors = fetched[0]
        pivot = row_of(factors, c)
        least = jnp.minimum(least, pivot[:1, :1])

        def step(x):
            kept = shrink(x * four(pivot))
            taken = shrink(factors * four(row_of(x, c)))
            return jnp.where(rows == c, x, settle(shrink(kept - taken + 17 * PRIME)))

        waiting = fetched[1:]
        if c + AHEAD < BLOCK:
            waiting.append(column_of(matrix, c + AHEAD))
        fetched = [step(x) for x in waiting]
        matrix = step(matrix)
    diagonal = lane_sum(jnp.where(rows == lanes, matrix, 0))
    scale = power(jnp.broadcast_to(diagonal, wide))
    out_ref[...] = mulmod(matrix, scale)[:, BLOCK : 2 * BLOCK].astype(f32)

    @pl.when(jnp.min(least.astype(f32)) == 0.0)
    def _():
        def eliminate(c, m):
            column = lane_sum(jnp.where(lanes == c, m, 0))
            row_ids = lax.broadcasted_iota(i32, (BLOCK, 1), 0)
            usable = (column != 0) & (row_ids >= c)
            at = jnp.min(jnp.where(usable, row_ids, BLOCK).astype(f32), axis=0, keepdims=True)
            at = to_int(at)
            at = jnp.where(at == BLOCK, c, at)
            at = jnp.broadcast_to(at, wide)
            pivot_row = jnp.broadcast_to(sublane_sum(jnp.where(rows == at, m, 0)), wide)
            current = jnp.broadcast_to(sublane_sum(jnp.where(rows == c, m, 0)), wide)
            swapped = jnp.where(rows == c, pivot_row, jnp.where(rows == at, current, m))
            pivot = jnp.broadcast_to(lane_sum(jnp.where(lanes == c, pivot_row, 0)), wide)
            scaled = mulmod(pivot_row, power(pivot))
            factors = jnp.broadcast_to(lane_sum(jnp.where(lanes == c, swapped, 0)), wide)
            reduced = settle(swapped - mulmod(factors, scaled) + PRIME)
            return jnp.where(rows == c, scaled, reduced)

        m = lax.fori_loop(0, BLOCK, eliminate, start)
        out_ref[...] = m[:, BLOCK : 2 * BLOCK].astype(f32)


def call(kernel, outs, args, smem=(), scratch=(), flops=0):
    specs = [
        pl.BlockSpec(memory_space=pltpu.SMEM if n in smem else pltpu.VMEM)
        for n in range(len(args))
    ]
    shapes = [jax.ShapeDtypeStruct(s, t) for s, t in outs]
    got = pl.pallas_call(
        kernel,
        out_shape=shapes,
        in_specs=specs,
        out_specs=[pl.BlockSpec(memory_space=pltpu.VMEM)] * len(shapes),
        scratch_shapes=list(scratch),
        compiler_params=pltpu.CompilerParams(vmem_limit_bytes=32 * 2**20),
        cost_estimate=pl.CostEstimate(flops=flops, bytes_accessed=4 * 2**20, transcendentals=0),
    )(*args)
    return got


def tile_at(t):
    return lax.rem(t, ROW_Y), place(lax.div(t, ROW_Y)) * BLOCK


def place(z):
    return (z & 1) * 4 + (z >> 1)


def forward(cols_ref, block_ref, tiles_ref, out_ref, count, slots):
    for r in range(count):
        total = None
        for s in range(0, slots, 2):
            pair = []
            for k in (s, s + 1):
                part, row = tile_at(cols_ref[r, k])
                pair.append(stack_digits(block_ref[part, pl.ds(pl.multiple_of(row, BLOCK), BLOCK), :]))
            at = r * slots + s
            stored = jnp.concatenate([tiles_ref[at], tiles_ref[at + 1]], axis=1)
            term = dot_t(jnp.concatenate(pair, axis=1), stored)
            total = term if total is None else total + term
        out_ref[r * BLOCK : (r + 1) * BLOCK, :] = fold_two(total[:BLOCK], total[BLOCK:])


def backward(cols_ref, projected, tiles_ref, sums_ref, out_ref, count, slots):
    sums_ref[...] = jnp.zeros_like(sums_ref)
    gram = jnp.zeros((BLOCK, BLOCK), f32)
    for r in range(count):
        stacked = stack_digits(projected[r])
        gram = gram + self_product(stacked)
        for s in range(0, slots, 2):
            at = r * slots + s
            terms = dot(stacked, jnp.concatenate([tiles_ref[at], tiles_ref[at + 1]], axis=1))
            sums_ref[cols_ref[r, s]] += terms[:, :TILE]
            sums_ref[cols_ref[r, s + 1]] += terms[:, TILE:]
    for t in range(ROWS):
        whole = sums_ref[t]
        y, z = t % ROW_Y, place(t // ROW_Y)
        out_ref[y, z * BLOCK : (z + 1) * BLOCK, :] = fold_two(whole[:BLOCK], whole[BLOCK:])
    packed = pack(modp(gram))
    for y in range(ROW_Y):
        out_ref[y, PART : PART + SMALL, :] = packed


def forward_first_kernel(count, slots, cols_ref, block_ref, entries_ref, out_ref, tiles_ref):
    for n in range(count * slots):
        tiles_ref[n] = entries_ref[n].astype(f32).astype(bf16)
    forward(cols_ref, block_ref, tiles_ref, out_ref, count, slots)


def forward_second_kernel(count, slots, cols_ref, block_ref, tiles_ref, out_ref):
    forward(cols_ref, block_ref, tiles_ref, out_ref, count, slots)
    square = block_ref[0, PART : PART + SMALL, :]
    for y in range(1, ROW_Y):
        square = square + block_ref[y, PART : PART + SMALL, :]
    out_ref[count * BLOCK : count * BLOCK + SMALL, :] = modp(square)


def over_parts(parts_ref, at):
    total = parts_ref[0, at, :]
    for k in range(1, parts_ref.shape[0]):
        total = total + parts_ref[k, at, :]
    return modp(total)


def backward_first_kernel(count, slots, cols_ref, parts_ref, tiles_ref, out_ref, y_ref, sums_ref):
    projected = []
    for r in range(count):
        at = slice(r * BLOCK, (r + 1) * BLOCK)
        value = over_parts(parts_ref, at)
        y_ref[at, :] = value
        projected.append(value)
    backward(cols_ref, projected, tiles_ref, sums_ref, out_ref, count, slots)


def backward_second_kernel(
    count, slots, cols_ref, parts_ref, tiles_ref, gram_ref, inv_y_ref, out_ref, both_ref, sums_ref
):
    small = slice(count * BLOCK, count * BLOCK + SMALL)
    square = unpack(over_parts(parts_ref, small))
    both = modp(square + gram_ref[...])
    both_ref[...] = both
    projected = []
    for r in range(count):
        at = slice(r * BLOCK, (r + 1) * BLOCK)
        value = over_parts(parts_ref, at)
        projected.append(modp(value - product(both, inv_y_ref[at, :]) + modulus))
    backward(cols_ref, projected, tiles_ref, sums_ref, out_ref, count, slots)


def sum_y_kernel(in_ref, out_ref):
    for z in range(ROW_Z):
        at = slice(z * BLOCK, (z + 1) * BLOCK)
        total = in_ref[0, at, :]
        for y in range(1, ROW_Y):
            total = total + in_ref[y, at, :]
        out_ref[z, :BLOCK, :] = total
    small = slice(PART, PART + SMALL)
    total = in_ref[0, small, :]
    for y in range(1, ROW_Y):
        total = total + in_ref[y, small, :]
    for z in range(ROW_Z):
        out_ref[z, BLOCK:, :] = total


def summed(in_ref):
    total = in_ref[0]
    for k in range(1, in_ref.shape[0]):
        total = total + in_ref[k]
    return modp(total)


def third_kernel(
    gram_ref, square_ref, inverse_ref, older_ref, now_ref, earlier_ref, earliest_ref, out_ref, float_inverse_ref, float_earlier_ref
):
    gram, inverse = gram_ref[...].astype(f32), inverse_ref[...].astype(f32)
    float_inverse_ref[...] = inverse
    float_earlier_ref[...] = earlier_ref[...].astype(f32)
    middle = modp(eye() - product(inverse, gram) + modulus)
    both = modp(square_ref[...].astype(f32) + gram)
    third = product(product(both, middle), older_ref[...].astype(f32))
    out_ref[...] = modp(now_ref[...] - product(third, earliest_ref[...].astype(f32)) + modulus)


def shift_kernel(in_ref, inverse_ref, earlier_ref, base_ref, out_ref, shifted_ref, gram_ref):
    total = summed(in_ref)
    applied = total[:BLOCK]
    gram = unpack(total[BLOCK:])
    gram_ref[...] = gram
    second = product(gram, inverse_ref[...])
    shifted = modp(applied + base_ref[...] + (modulus - product(second, earlier_ref[...])))
    shifted_ref[...] = shifted
    square = pack(self_product(stack_digits(applied)))
    for z in range(ROW_Z):
        out_ref[z, :BLOCK, :] = shifted
        out_ref[z, BLOCK:, :] = square


def spread_y_kernel(in_ref, out_ref):
    square = in_ref[0, BLOCK:, :]
    for z in range(1, ROW_Z):
        square = square + in_ref[z, BLOCK:, :]
    square = modp(square)
    for y in range(ROW_Y):
        for z in range(ROW_Z):
            out_ref[y, z * BLOCK : (z + 1) * BLOCK, :] = in_ref[z, :BLOCK, :]
        out_ref[y, PART:, :] = square


def inverse_kernel(
    count, gram_ref, older_ref, y_ref, now_ref, earlier_ref, inv_y_ref, inv_x_ref, old_ref, inverse_ref
):
    gram = gram_ref[...]
    invert(gram, inverse_ref)
    inverse = inverse_ref[...]
    for r in range(count):
        at = slice(r * BLOCK, (r + 1) * BLOCK)
        inv_y_ref[at, :] = product(inverse, y_ref[at, :])
    inv_x_ref[...] = product(inverse, now_ref[...])
    middle = modp(eye() - product(inverse, gram) + modulus)
    old_ref[...] = product(product(middle, older_ref[...]), earlier_ref[...])


def ending_kernel(
    in_ref, both_ref, shifted_ref, inv_x_ref, old_ref, out_ref, result_ref, base_ref, gram_ref, inverse_ref, inv_next_ref
):
    total = summed(in_ref)
    applied = total[:BLOCK]
    gram = unpack(total[BLOCK:])
    gram_ref[...] = gram
    square = pack(self_product(stack_digits(applied)))
    for k in range(out_ref.shape[0]):
        out_ref[k] = square
    both = both_ref[...]
    following = modp(shifted_ref[...] - product(both, inv_x_ref[...]) + modulus)
    result_ref[...] = following / modulus
    minus = modp(product(gram, inv_x_ref[...]) + product(both, old_ref[...]))
    base_ref[...] = modp(applied + following + (modulus - minus))
    invert(gram, inverse_ref)
    inv_next_ref[...] = product(inverse_ref[...], following)


def relay_kernel(in_ref, out_ref):
    total = summed(in_ref)
    for k in range(out_ref.shape[0]):
        out_ref[k] = total


def last_kernel(in_ref, gram_ref, base_ref, inv_next_ref, out_ref):
    both = modp(unpack(summed(in_ref)) + gram_ref[...])
    out_ref[...] = modp(base_ref[...] - product(both, inv_next_ref[...]) + modulus) / modulus


def exchange(parts, axis):
    return lax.all_to_all(parts, axis, 0, 0, tiled=True)


def flip(x, axis):
    return lax.ppermute(x, axis, [(0, 1), (1, 0)])


def together(*arrays):
    return lax.optimization_barrier(arrays)


def spread_x(part):
    return exchange(jnp.broadcast_to(part[None], (COL_X, *part.shape)), "x")


def body(entries, tile_cols, block_now, block_prev, block_prev2, gram_prev, square_prev, inverse_prev, inverse_prev2):
    count, slots = tile_cols.shape
    length = count * BLOCK
    stored = entries.reshape(count * slots, TILE, TILE)
    current = block_now.astype(f32)
    shard = (BLOCK, TILE)
    small = (BLOCK, BLOCK)
    sums = [pltpu.VMEM((ROWS, 2 * BLOCK, TILE), f32)]

    along_z = exchange(jnp.broadcast_to(current[None], (ROW_Z, *shard)), Z_LO)
    block = exchange(jnp.broadcast_to(along_z.reshape(1, PART, TILE), (ROW_Y, PART, TILE)), "y")
    partial, tiles = call(
        functools.partial(forward_first_kernel, count, slots),
        [((length, TILE), f32), (stored.shape, bf16)], [tile_cols, block, stored], smem=(0,),
    )
    other = flip(partial, "zh")
    partial, *given = together(
        partial, gram_prev, square_prev, inverse_prev, inverse_prev2, current, block_prev, block_prev2
    )
    base, inverse_old, earlier = call(
        third_kernel, [(shard, f32), (small, f32), (shard, f32)], given, flops=10**9
    )
    other, base, inverse_old, earlier = together(other, base, inverse_old, earlier)
    pair = partial + other
    parts = spread_x(pair + flip(pair, "c"))

    spread, projected = call(
        functools.partial(backward_first_kernel, count, slots),
        [((ROW_Y, PART + SMALL, TILE), f32), ((length, TILE), f32)],
        [tile_cols, parts, tiles], smem=(0,), scratch=sums,
    )
    chunks = (ROW_Z, BLOCK + SMALL, TILE)
    [by_z] = call(sum_y_kernel, [(chunks, f32)], [exchange(spread, "y")])
    out, shifted, gram_now = call(
        shift_kernel, [(chunks, f32), (shard, f32), (small, f32)],
        [exchange(by_z, Z_LO), inverse_old, earlier, base],
    )

    [spread] = call(spread_y_kernel, [((ROW_Y, PART + SMALL, TILE), f32)], [exchange(out, Z_LO)])
    [partial] = call(
        functools.partial(forward_second_kernel, count, slots),
        [((length + SMALL, TILE), f32)], [tile_cols, exchange(spread, "y"), tiles], smem=(0,),
    )
    other = flip(partial, "zh")
    partial, gram_now = together(partial, gram_now)
    inv_y, inv_x, old, inverse_now = call(
        functools.partial(inverse_kernel, count),
        [((length, TILE), f32), (shard, f32), (shard, f32), (small, f32)],
        [gram_now, inverse_old, projected, current, earlier],
        flops=10**9,
    )
    other, inv_y, inv_x, old = together(other, inv_y, inv_x, old)
    pair = partial + other
    parts = spread_x(pair + flip(pair, "c"))
    spread, both = call(
        functools.partial(backward_second_kernel, count, slots),
        [((ROW_Y, PART + SMALL, TILE), f32), (small, f32)],
        [tile_cols, parts, tiles, gram_now, inv_y], smem=(0,), scratch=sums,
    )
    [by_z] = call(sum_y_kernel, [(chunks, f32)], [exchange(spread, "y")])
    near = ROW_Y * COL_X * COL_C
    far = COL_Z * ROW_Z
    out, result, base, gram_next, inverse_next, inv_next = call(
        ending_kernel,
        [((near, SMALL, TILE), f32), (shard, f32), (shard, f32), (small, f32), (small, f32), (shard, f32)],
        [exchange(by_z, Z_LO), both, shifted, inv_x, old],
    )
    [out] = call(relay_kernel, [((far, SMALL, TILE), f32)], [exchange(out, ("y", "x", "c"))])
    [later] = call(last_kernel, [(shard, f32)], [exchange(out, ("zh", *Z_LO)), gram_next, base, inv_next])
    return result, later


def solution(mesh):
    fine = Mesh(mesh.devices.reshape(2, 2, 2, ROW_Y, COL_Z, COL_X, COL_C), ("z2", "z1", "z0", "y", "zh", "x", "c"))
    row, col = ("z2", "z1", "z0", "y"), ("zh", "x", "c")
    columns = P(None, (*col, *row))
    return jax.shard_map(
        body,
        mesh=fine,
        in_specs=(P(row, col, None, None), P(row, col), columns, columns, columns, P(), P(), P(), P()),
        out_specs=(columns, columns),
        check_vma=False,
    )
```

```python
import functools

import jax
import jax.numpy as jnp
from jax import lax
from jax.experimental import pallas as pl
from jax.experimental.pallas import tpu as pltpu
from jax.sharding import Mesh
from jax.sharding import PartitionSpec as P

PRIME = 65521
modulus = 65521.0
BLOCK = 32
TILE = 128
ROW_Z, ROW_Y = 8, 4
COL_Z, COL_X, COL_C = 2, 4, 2
Z_LO = ("z0", "z2", "z1")
ROWS = ROW_Z * ROW_Y
AHEAD = 3
SMALL = 8
PART = ROW_Z * BLOCK

f32, bf16, i32 = jnp.float32, jnp.bfloat16, jnp.int32


def modp(x):
    top = jnp.floor(x * (1.0 / 65536.0))
    rest = x - top * modulus
    return jnp.where(rest >= modulus, rest - modulus, rest)


def digits(x):
    top = jnp.floor(x * (1.0 / 256.0))
    return top, x - top * 256.0


def stack_digits(x):
    top, low = digits(x)
    return jnp.concatenate([top, low], axis=0).astype(bf16)


def fold_two(top, low):
    return modp(modp(modp(top) * 256.0) + low)


def fold_three(upper, middle, lower):
    return modp(modp(upper) * 15.0 + modp(modp(middle) * 256.0) + lower)


def dot(a, b):
    return lax.dot_general(a, b, (((1,), (0,)), ((), ())), preferred_element_type=f32)


def dot_t(a, b):
    return lax.dot_general(a, b, (((1,), (1,)), ((), ())), preferred_element_type=f32)


def product(left, right):
    stacked = stack_digits(left)
    top, low = digits(right)
    by_top = dot(stacked, top.astype(bf16))
    by_low = dot(stacked, low.astype(bf16))
    return fold_three(by_top[:BLOCK], by_top[BLOCK:] + by_low[:BLOCK], by_low[BLOCK:])


def self_product(stacked):
    all_four = dot_t(stacked, stacked)
    by_top = all_four[:, :BLOCK]
    by_low = all_four[:, BLOCK:]
    return fold_three(by_top[:BLOCK], by_top[BLOCK:] + by_low[:BLOCK], by_low[BLOCK:])


def pack(matrix):
    return jnp.concatenate([matrix[8 * k : 8 * k + 8] for k in range(4)], axis=1)


def unpack(packed):
    return jnp.concatenate([packed[:, 32 * k : 32 * k + 32] for k in range(4)], axis=0)


def eye():
    rows = lax.broadcasted_iota(i32, (BLOCK, BLOCK), 0)
    cols = lax.broadcasted_iota(i32, (BLOCK, BLOCK), 1)
    return (rows == cols).astype(f32)


def shrink(x):
    return x - lax.shift_right_logical(x, 16) * PRIME


def settle(x):
    less = x - PRIME
    return jnp.where(less < 0, x, less)


def mulmod(a, b):
    return settle(shrink(shrink(a * b)))


def power(a):
    def fourth_up(x):
        for unused in range(4):
            x = mulmod(x, x)
        return x

    a2 = mulmod(a, a)
    a3 = mulmod(a2, a)
    a6 = mulmod(a3, a3)
    a12 = mulmod(a6, a6)
    a14 = mulmod(a12, a2)
    a15 = mulmod(a12, a3)
    a255 = mulmod(fourth_up(a15), a15)
    high = mulmod(fourth_up(a255), a14)
    return mulmod(fourth_up(high), a15)


def to_int(x):
    return x.astype(i32)


def lane_sum(x):
    return to_int(jnp.sum(x.astype(f32), axis=1, keepdims=True))


def sublane_sum(x):
    return to_int(jnp.sum(x.astype(f32), axis=0, keepdims=True))


def invert(gram, out_ref):
    wide = (BLOCK, 128)
    rows = lax.broadcasted_iota(i32, wide, 0)
    lanes = lax.broadcasted_iota(i32, wide, 1)
    start = jnp.concatenate([gram, eye(), jnp.zeros((BLOCK, 64), f32)], axis=1)
    start = to_int(start)

    def four(x):
        return jnp.concatenate([x] * 4, axis=0)

    def row_of(x, c):
        return jnp.broadcast_to(x[c : c + 1], (8, 128))

    def column_of(x, c):
        return jnp.broadcast_to(x[:, c : c + 1], wide)

    matrix = start
    least = jnp.full((1, 1), PRIME, i32)
    fetched = [column_of(matrix, c) for c in range(AHEAD)]
    for c in range(BLOCK):
        factors = fetched[0]
        pivot = row_of(factors, c)
        least = jnp.minimum(least, pivot[:1, :1])

        def step(x):
            kept = shrink(x * four(pivot))
            taken = shrink(factors * four(row_of(x, c)))
            return jnp.where(rows == c, x, settle(shrink(kept - taken + 17 * PRIME)))

        waiting = fetched[1:]
        if c + AHEAD < BLOCK:
            waiting.append(column_of(matrix, c + AHEAD))
        fetched = [step(x) for x in waiting]
        matrix = step(matrix)
    diagonal = lane_sum(jnp.where(rows == lanes, matrix, 0))
    scale = power(jnp.broadcast_to(diagonal, wide))
    out_ref[...] = mulmod(matrix, scale)[:, BLOCK : 2 * BLOCK].astype(f32)

    @pl.when(jnp.min(least.astype(f32)) == 0.0)
    def _():
        def eliminate(c, m):
            column = lane_sum(jnp.where(lanes == c, m, 0))
            row_ids = lax.broadcasted_iota(i32, (BLOCK, 1), 0)
            usable = (column != 0) & (row_ids >= c)
            at = jnp.min(jnp.where(usable, row_ids, BLOCK).astype(f32), axis=0, keepdims=True)
            at = to_int(at)
            at = jnp.where(at == BLOCK, c, at)
            at = jnp.broadcast_to(at, wide)
            pivot_row = jnp.broadcast_to(sublane_sum(jnp.where(rows == at, m, 0)), wide)
            current = jnp.broadcast_to(sublane_sum(jnp.where(rows == c, m, 0)), wide)
            swapped = jnp.where(rows == c, pivot_row, jnp.where(rows == at, current, m))
            pivot = jnp.broadcast_to(lane_sum(jnp.where(lanes == c, pivot_row, 0)), wide)
            scaled = mulmod(pivot_row, power(pivot))
            factors = jnp.broadcast_to(lane_sum(jnp.where(lanes == c, swapped, 0)), wide)
            reduced = settle(swapped - mulmod(factors, scaled) + PRIME)
            return jnp.where(rows == c, scaled, reduced)

        m = lax.fori_loop(0, BLOCK, eliminate, start)
        out_ref[...] = m[:, BLOCK : 2 * BLOCK].astype(f32)


def call(kernel, outs, args, smem=(), scratch=(), flops=0):
    specs = [
        pl.BlockSpec(memory_space=pltpu.SMEM if n in smem else pltpu.VMEM)
        for n in range(len(args))
    ]
    shapes = [jax.ShapeDtypeStruct(s, t) for s, t in outs]
    got = pl.pallas_call(
        kernel,
        out_shape=shapes,
        in_specs=specs,
        out_specs=[pl.BlockSpec(memory_space=pltpu.VMEM)] * len(shapes),
        scratch_shapes=list(scratch),
        compiler_params=pltpu.CompilerParams(vmem_limit_bytes=32 * 2**20),
        cost_estimate=pl.CostEstimate(flops=flops, bytes_accessed=4 * 2**20, transcendentals=0),
    )(*args)
    return got


def tile_at(t):
    return across(lax.rem(t, ROW_Y)), place(lax.div(t, ROW_Y)) * BLOCK


def place(z):
    return (z & 1) * 4 + (z >> 1)


def across(y):
    return (y & 1) * 2 + (y >> 1)


def forward(cols_ref, block_ref, tiles_ref, out_ref, count, slots):
    for r in range(count):
        total = None
        for s in range(0, slots, 2):
            pair = []
            for k in (s, s + 1):
                part, row = tile_at(cols_ref[r, k])
                pair.append(stack_digits(block_ref[part, pl.ds(pl.multiple_of(row, BLOCK), BLOCK), :]))
            at = r * slots + s
            stored = jnp.concatenate([tiles_ref[at], tiles_ref[at + 1]], axis=1)
            term = dot_t(jnp.concatenate(pair, axis=1), stored)
            total = term if total is None else total + term
        out_ref[r * BLOCK : (r + 1) * BLOCK, :] = fold_two(total[:BLOCK], total[BLOCK:])


def backward(cols_ref, projected, tiles_ref, sums_ref, out_ref, count, slots):
    sums_ref[...] = jnp.zeros_like(sums_ref)
    gram = jnp.zeros((BLOCK, BLOCK), f32)
    for r in range(count):
        stacked = stack_digits(projected[r])
        gram = gram + self_product(stacked)
        for s in range(0, slots, 2):
            at = r * slots + s
            terms = dot(stacked, jnp.concatenate([tiles_ref[at], tiles_ref[at + 1]], axis=1))
            sums_ref[cols_ref[r, s]] += terms[:, :TILE]
            sums_ref[cols_ref[r, s + 1]] += terms[:, TILE:]
    for t in range(ROWS):
        whole = sums_ref[t]
        y, z = across(t % ROW_Y), place(t // ROW_Y)
        out_ref[y, z * BLOCK : (z + 1) * BLOCK, :] = fold_two(whole[:BLOCK], whole[BLOCK:])
    packed = pack(modp(gram))
    for y in range(ROW_Y):
        out_ref[y, PART : PART + SMALL, :] = packed


def forward_first_kernel(count, slots, cols_ref, block_ref, entries_ref, out_ref, tiles_ref):
    for n in range(count * slots):
        tiles_ref[n] = entries_ref[n].astype(f32).astype(bf16)
    forward(cols_ref, block_ref, tiles_ref, out_ref, count, slots)


def forward_second_kernel(count, slots, cols_ref, block_ref, tiles_ref, out_ref):
    forward(cols_ref, block_ref, tiles_ref, out_ref, count, slots)
    square = block_ref[0, PART : PART + SMALL, :]
    for y in range(1, ROW_Y):
        square = square + block_ref[y, PART : PART + SMALL, :]
    out_ref[count * BLOCK : count * BLOCK + SMALL, :] = modp(square)


def over_parts(parts_ref, at):
    total = parts_ref[0, at, :]
    for k in range(1, parts_ref.shape[0]):
        total = total + parts_ref[k, at, :]
    return modp(total)


def backward_first_kernel(count, slots, cols_ref, parts_ref, tiles_ref, out_ref, y_ref, sums_ref):
    projected = []
    for r in range(count):
        at = slice(r * BLOCK, (r + 1) * BLOCK)
        value = over_parts(parts_ref, at)
        y_ref[at, :] = value
        projected.append(value)
    backward(cols_ref, projected, tiles_ref, sums_ref, out_ref, count, slots)


def backward_second_kernel(
    count, slots, cols_ref, parts_ref, tiles_ref, gram_ref, inv_y_ref, out_ref, both_ref, sums_ref
):
    small = slice(count * BLOCK, count * BLOCK + SMALL)
    square = unpack(over_parts(parts_ref, small))
    both = modp(square + gram_ref[...])
    both_ref[...] = both
    projected = []
    for r in range(count):
        at = slice(r * BLOCK, (r + 1) * BLOCK)
        value = over_parts(parts_ref, at)
        projected.append(modp(value - product(both, inv_y_ref[at, :]) + modulus))
    backward(cols_ref, projected, tiles_ref, sums_ref, out_ref, count, slots)


def sum_y_kernel(in_ref, out_ref):
    for z in range(ROW_Z):
        at = slice(z * BLOCK, (z + 1) * BLOCK)
        total = in_ref[0, at, :]
        for y in range(1, ROW_Y):
            total = total + in_ref[y, at, :]
        out_ref[z, :BLOCK, :] = total
    small = slice(PART, PART + SMALL)
    total = in_ref[0, small, :]
    for y in range(1, ROW_Y):
        total = total + in_ref[y, small, :]
    for z in range(ROW_Z):
        out_ref[z, BLOCK:, :] = total


def summed(in_ref):
    total = in_ref[0]
    for k in range(1, in_ref.shape[0]):
        total = total + in_ref[k]
    return modp(total)


def third_kernel(
    gram_ref, square_ref, inverse_ref, older_ref, now_ref, earlier_ref, earliest_ref, out_ref, float_inverse_ref, float_earlier_ref
):
    gram, inverse = gram_ref[...].astype(f32), inverse_ref[...].astype(f32)
    float_inverse_ref[...] = inverse
    float_earlier_ref[...] = earlier_ref[...].astype(f32)
    middle = modp(eye() - product(inverse, gram) + modulus)
    both = modp(square_ref[...].astype(f32) + gram)
    third = product(product(both, middle), older_ref[...].astype(f32))
    out_ref[...] = modp(now_ref[...] - product(third, earliest_ref[...].astype(f32)) + modulus)


def shift_kernel(in_ref, inverse_ref, earlier_ref, base_ref, out_ref, shifted_ref, gram_ref):
    total = summed(in_ref)
    applied = total[:BLOCK]
    gram = unpack(total[BLOCK:])
    gram_ref[...] = gram
    second = product(gram, inverse_ref[...])
    shifted = modp(applied + base_ref[...] + (modulus - product(second, earlier_ref[...])))
    shifted_ref[...] = shifted
    square = pack(self_product(stack_digits(applied)))
    for z in range(ROW_Z):
        out_ref[z, :BLOCK, :] = shifted
        out_ref[z, BLOCK:, :] = square


def spread_y_kernel(in_ref, out_ref):
    square = in_ref[0, BLOCK:, :]
    for z in range(1, ROW_Z):
        square = square + in_ref[z, BLOCK:, :]
    square = modp(square)
    for y in range(ROW_Y):
        for z in range(ROW_Z):
            out_ref[y, z * BLOCK : (z + 1) * BLOCK, :] = in_ref[z, :BLOCK, :]
        out_ref[y, PART:, :] = square


def inverse_kernel(
    count, gram_ref, older_ref, y_ref, now_ref, earlier_ref, inv_y_ref, inv_x_ref, old_ref, inverse_ref
):
    gram = gram_ref[...]
    invert(gram, inverse_ref)
    inverse = inverse_ref[...]
    for r in range(count):
        at = slice(r * BLOCK, (r + 1) * BLOCK)
        inv_y_ref[at, :] = product(inverse, y_ref[at, :])
    inv_x_ref[...] = product(inverse, now_ref[...])
    middle = modp(eye() - product(inverse, gram) + modulus)
    old_ref[...] = product(product(middle, older_ref[...]), earlier_ref[...])


def ending_kernel(
    in_ref, both_ref, shifted_ref, inv_x_ref, old_ref, out_ref, result_ref, base_ref, gram_ref, inverse_ref, inv_next_ref
):
    total = summed(in_ref)
    applied = total[:BLOCK]
    gram = unpack(total[BLOCK:])
    gram_ref[...] = gram
    square = pack(self_product(stack_digits(applied)))
    for k in range(out_ref.shape[0]):
        out_ref[k] = square
    both = both_ref[...]
    following = modp(shifted_ref[...] - product(both, inv_x_ref[...]) + modulus)
    result_ref[...] = following / modulus
    minus = modp(product(gram, inv_x_ref[...]) + product(both, old_ref[...]))
    base_ref[...] = modp(applied + following + (modulus - minus))
    invert(gram, inverse_ref)
    inv_next_ref[...] = product(inverse_ref[...], following)


def relay_kernel(in_ref, out_ref):
    total = summed(in_ref)
    for k in range(out_ref.shape[0]):
        out_ref[k] = total


def last_kernel(in_ref, gram_ref, base_ref, inv_next_ref, out_ref):
    both = modp(unpack(summed(in_ref)) + gram_ref[...])
    out_ref[...] = modp(base_ref[...] - product(both, inv_next_ref[...]) + modulus) / modulus


def exchange(parts, axis):
    return lax.all_to_all(parts, axis, 0, 0, tiled=True)


def flip(x, axis):
    return lax.ppermute(x, axis, [(0, 1), (1, 0)])


def together(*arrays):
    return lax.optimization_barrier(arrays)


def spread_x(part):
    return exchange(jnp.broadcast_to(part[None], (COL_X, *part.shape)), ("x0", "x1"))


def body(entries, tile_cols, block_now, block_prev, block_prev2, gram_prev, square_prev, inverse_prev, inverse_prev2):
    count, slots = tile_cols.shape
    length = count * BLOCK
    stored = entries.reshape(count * slots, TILE, TILE)
    current = block_now.astype(f32)
    shard = (BLOCK, TILE)
    small = (BLOCK, BLOCK)
    sums = [pltpu.VMEM((ROWS, 2 * BLOCK, TILE), f32)]

    along_z = exchange(jnp.broadcast_to(current[None], (ROW_Z, *shard)), Z_LO)
    block = exchange(jnp.broadcast_to(along_z.reshape(1, PART, TILE), (ROW_Y, PART, TILE)), ("y0", "y1"))
    partial, tiles = call(
        functools.partial(forward_first_kernel, count, slots),
        [((length, TILE), f32), (stored.shape, bf16)], [tile_cols, block, stored], smem=(0,),
    )
    other = flip(partial, "zh")
    partial, *given = together(
        partial, gram_prev, square_prev, inverse_prev, inverse_prev2, current, block_prev, block_prev2
    )
    base, inverse_old, earlier = call(
        third_kernel, [(shard, f32), (small, f32), (shard, f32)], given, flops=10**9
    )
    other, base, inverse_old, earlier = together(other, base, inverse_old, earlier)
    pair = partial + other
    parts = spread_x(pair + flip(pair, "c"))

    spread, projected = call(
        functools.partial(backward_first_kernel, count, slots),
        [((ROW_Y, PART + SMALL, TILE), f32), ((length, TILE), f32)],
        [tile_cols, parts, tiles], smem=(0,), scratch=sums,
    )
    chunks = (ROW_Z, BLOCK + SMALL, TILE)
    [by_z] = call(sum_y_kernel, [(chunks, f32)], [exchange(spread, ("y0", "y1"))])
    out, shifted, gram_now = call(
        shift_kernel, [(chunks, f32), (shard, f32), (small, f32)],
        [exchange(by_z, Z_LO), inverse_old, earlier, base],
    )

    [spread] = call(spread_y_kernel, [((ROW_Y, PART + SMALL, TILE), f32)], [exchange(out, Z_LO)])
    [partial] = call(
        functools.partial(forward_second_kernel, count, slots),
        [((length + SMALL, TILE), f32)], [tile_cols, exchange(spread, ("y0", "y1")), tiles], smem=(0,),
    )
    other = flip(partial, "zh")
    partial, gram_now = together(partial, gram_now)
    inv_y, inv_x, old, inverse_now = call(
        functools.partial(inverse_kernel, count),
        [((length, TILE), f32), (shard, f32), (shard, f32), (small, f32)],
        [gram_now, inverse_old, projected, current, earlier],
        flops=10**9,
    )
    other, inv_y, inv_x, old = together(other, inv_y, inv_x, old)
    pair = partial + other
    parts = spread_x(pair + flip(pair, "c"))
    spread, both = call(
        functools.partial(backward_second_kernel, count, slots),
        [((ROW_Y, PART + SMALL, TILE), f32), (small, f32)],
        [tile_cols, parts, tiles, gram_now, inv_y], smem=(0,), scratch=sums,
    )
    [by_z] = call(sum_y_kernel, [(chunks, f32)], [exchange(spread, ("y0", "y1"))])
    near = ROW_Y * COL_X * COL_C
    far = COL_Z * ROW_Z
    out, result, base, gram_next, inverse_next, inv_next = call(
        ending_kernel,
        [((near, SMALL, TILE), f32), (shard, f32), (shard, f32), (small, f32), (small, f32), (shard, f32)],
        [exchange(by_z, Z_LO), both, shifted, inv_x, old],
    )
    [out] = call(relay_kernel, [((far, SMALL, TILE), f32)], [exchange(out, ("y0", "y1", "x0", "x1", "c"))])
    [later] = call(last_kernel, [(shard, f32)], [exchange(out, ("zh", *Z_LO)), gram_next, base, inv_next])
    return result, later


def solution(mesh):
    fine = Mesh(mesh.devices.reshape(2, 2, 2, 2, 2, COL_Z, 2, 2, COL_C), ("z2", "z1", "z0", "y1", "y0", "zh", "x1", "x0", "c"))
    row, col = ("z2", "z1", "z0", "y1", "y0"), ("zh", "x1", "x0", "c")
    columns = P(None, (*col, *row))
    return jax.shard_map(
        body,
        mesh=fine,
        in_specs=(P(row, col, None, None), P(row, col), columns, columns, columns, P(), P(), P(), P()),
        out_specs=(columns, columns),
        check_vma=False,
    )
```

```python
import functools

import jax
import jax.numpy as jnp
from jax import lax
from jax.experimental import pallas as pl
from jax.experimental.pallas import tpu as pltpu
from jax.sharding import Mesh
from jax.sharding import PartitionSpec as P

PRIME = 65521
modulus = 65521.0
BLOCK = 32
TILE = 128
ROW_Z, ROW_Y = 8, 4
COL_Z, COL_X, COL_C = 2, 4, 2
Z_LO = ("z0", "z2", "z1")
ROWS = ROW_Z * ROW_Y
AHEAD = 3
SMALL = 8
PART = ROW_Z * BLOCK

f32, bf16, i32 = jnp.float32, jnp.bfloat16, jnp.int32


def modp(x):
    top = jnp.floor(x * (1.0 / 65536.0))
    rest = x - top * modulus
    return jnp.where(rest >= modulus, rest - modulus, rest)


def near(x):
    return x - jnp.floor(x * (1.0 / 65536.0)) * modulus


def digits(x):
    top = jnp.floor(x * (1.0 / 256.0))
    return top, x - top * 256.0


def stack_digits(x):
    top, low = digits(x)
    return jnp.concatenate([top, low], axis=0).astype(bf16)


def fold_two(top, low):
    return modp(near(near(top) * 256.0) + low)


def fold_three(upper, middle, lower):
    return modp(near(upper) * 15.0 + near(modp(middle) * 256.0) + lower)


def dot(a, b):
    return lax.dot_general(a, b, (((1,), (0,)), ((), ())), preferred_element_type=f32)


def dot_t(a, b):
    return lax.dot_general(a, b, (((1,), (1,)), ((), ())), preferred_element_type=f32)


def product(left, right):
    stacked = stack_digits(left)
    top, low = digits(right)
    by_top = dot(stacked, top.astype(bf16))
    by_low = dot(stacked, low.astype(bf16))
    return fold_three(by_top[:BLOCK], by_top[BLOCK:] + by_low[:BLOCK], by_low[BLOCK:])


def self_product(stacked):
    all_four = dot_t(stacked, stacked)
    by_top = all_four[:, :BLOCK]
    by_low = all_four[:, BLOCK:]
    return fold_three(by_top[:BLOCK], by_top[BLOCK:] + by_low[:BLOCK], by_low[BLOCK:])


def pack(matrix):
    return jnp.concatenate([matrix[8 * k : 8 * k + 8] for k in range(4)], axis=1)


def unpack(packed):
    return jnp.concatenate([packed[:, 32 * k : 32 * k + 32] for k in range(4)], axis=0)


def eye():
    rows = lax.broadcasted_iota(i32, (BLOCK, BLOCK), 0)
    cols = lax.broadcasted_iota(i32, (BLOCK, BLOCK), 1)
    return (rows == cols).astype(f32)


def shrink(x):
    return x - lax.shift_right_logical(x, 16) * PRIME


def settle(x):
    less = x - PRIME
    return jnp.where(less < 0, x, less)


def mulmod(a, b):
    return settle(shrink(shrink(a * b)))


def power(a):
    def fourth_up(x):
        for unused in range(4):
            x = mulmod(x, x)
        return x

    a2 = mulmod(a, a)
    a3 = mulmod(a2, a)
    a6 = mulmod(a3, a3)
    a12 = mulmod(a6, a6)
    a14 = mulmod(a12, a2)
    a15 = mulmod(a12, a3)
    a255 = mulmod(fourth_up(a15), a15)
    high = mulmod(fourth_up(a255), a14)
    return mulmod(fourth_up(high), a15)


def to_int(x):
    return x.astype(i32)


def lane_sum(x):
    return to_int(jnp.sum(x.astype(f32), axis=1, keepdims=True))


def sublane_sum(x):
    return to_int(jnp.sum(x.astype(f32), axis=0, keepdims=True))


def invert(gram, out_ref):
    wide = (BLOCK, 128)
    rows = lax.broadcasted_iota(i32, wide, 0)
    lanes = lax.broadcasted_iota(i32, wide, 1)
    start = jnp.concatenate([gram, eye(), jnp.zeros((BLOCK, 64), f32)], axis=1)
    start = to_int(start)

    def four(x):
        return jnp.concatenate([x] * 4, axis=0)

    def row_of(x, c):
        return jnp.broadcast_to(x[c : c + 1], (8, 128))

    def column_of(x, c):
        return jnp.broadcast_to(x[:, c : c + 1], wide)

    matrix = start
    least = jnp.full((1, 1), PRIME, i32)
    fetched = [column_of(matrix, c) for c in range(AHEAD)]
    for c in range(BLOCK):
        factors = fetched[0]
        pivot = row_of(factors, c)
        least = jnp.minimum(least, pivot[:1, :1])

        def step(x):
            kept = shrink(x * four(pivot))
            taken = shrink(factors * four(row_of(x, c)))
            return jnp.where(rows == c, x, settle(shrink(kept - taken + 17 * PRIME)))

        waiting = fetched[1:]
        if c + AHEAD < BLOCK:
            waiting.append(column_of(matrix, c + AHEAD))
        fetched = [step(x) for x in waiting]
        matrix = step(matrix)
    diagonal = lane_sum(jnp.where(rows == lanes, matrix, 0))
    scale = power(jnp.broadcast_to(diagonal, wide))
    out_ref[...] = mulmod(matrix, scale)[:, BLOCK : 2 * BLOCK].astype(f32)

    @pl.when(jnp.min(least.astype(f32)) == 0.0)
    def _():
        def eliminate(c, m):
            column = lane_sum(jnp.where(lanes == c, m, 0))
            row_ids = lax.broadcasted_iota(i32, (BLOCK, 1), 0)
            usable = (column != 0) & (row_ids >= c)
            at = jnp.min(jnp.where(usable, row_ids, BLOCK).astype(f32), axis=0, keepdims=True)
            at = to_int(at)
            at = jnp.where(at == BLOCK, c, at)
            at = jnp.broadcast_to(at, wide)
            pivot_row = jnp.broadcast_to(sublane_sum(jnp.where(rows == at, m, 0)), wide)
            current = jnp.broadcast_to(sublane_sum(jnp.where(rows == c, m, 0)), wide)
            swapped = jnp.where(rows == c, pivot_row, jnp.where(rows == at, current, m))
            pivot = jnp.broadcast_to(lane_sum(jnp.where(lanes == c, pivot_row, 0)), wide)
            scaled = mulmod(pivot_row, power(pivot))
            factors = jnp.broadcast_to(lane_sum(jnp.where(lanes == c, swapped, 0)), wide)
            reduced = settle(swapped - mulmod(factors, scaled) + PRIME)
            return jnp.where(rows == c, scaled, reduced)

        m = lax.fori_loop(0, BLOCK, eliminate, start)
        out_ref[...] = m[:, BLOCK : 2 * BLOCK].astype(f32)


def call(kernel, outs, args, smem=(), scratch=(), flops=0):
    specs = [
        pl.BlockSpec(memory_space=pltpu.SMEM if n in smem else pltpu.VMEM)
        for n in range(len(args))
    ]
    shapes = [jax.ShapeDtypeStruct(s, t) for s, t in outs]
    got = pl.pallas_call(
        kernel,
        out_shape=shapes,
        in_specs=specs,
        out_specs=[pl.BlockSpec(memory_space=pltpu.VMEM)] * len(shapes),
        scratch_shapes=list(scratch),
        compiler_params=pltpu.CompilerParams(vmem_limit_bytes=32 * 2**20),
        cost_estimate=pl.CostEstimate(flops=flops, bytes_accessed=4 * 2**20, transcendentals=0),
    )(*args)
    return got


def tile_at(t):
    return across(lax.rem(t, ROW_Y)), place(lax.div(t, ROW_Y)) * BLOCK


def place(z):
    return (z & 1) * 4 + (z >> 1)


def across(y):
    return (y & 1) * 2 + (y >> 1)


def forward(cols_ref, block_ref, tiles_ref, out_ref, count, slots):
    for r in range(count):
        total = None
        for s in range(0, slots, 2):
            pair = []
            for k in (s, s + 1):
                part, row = tile_at(cols_ref[r, k])
                pair.append(stack_digits(block_ref[part, pl.ds(pl.multiple_of(row, BLOCK), BLOCK), :]))
            at = r * slots + s
            stored = jnp.concatenate([tiles_ref[at], tiles_ref[at + 1]], axis=1)
            term = dot_t(jnp.concatenate(pair, axis=1), stored)
            total = term if total is None else total + term
        out_ref[r * BLOCK : (r + 1) * BLOCK, :] = fold_two(total[:BLOCK], total[BLOCK:])


def backward(cols_ref, projected, tiles_ref, sums_ref, out_ref, count, slots):
    sums_ref[...] = jnp.zeros_like(sums_ref)
    gram = jnp.zeros((BLOCK, BLOCK), f32)
    for r in range(count):
        stacked = stack_digits(projected[r])
        gram = gram + self_product(stacked)
        for s in range(0, slots, 2):
            at = r * slots + s
            terms = dot(stacked, jnp.concatenate([tiles_ref[at], tiles_ref[at + 1]], axis=1))
            sums_ref[cols_ref[r, s]] += terms[:, :TILE]
            sums_ref[cols_ref[r, s + 1]] += terms[:, TILE:]
    for t in range(ROWS):
        whole = sums_ref[t]
        y, z = across(t % ROW_Y), place(t // ROW_Y)
        out_ref[y, z * BLOCK : (z + 1) * BLOCK, :] = fold_two(whole[:BLOCK], whole[BLOCK:])
    packed = pack(modp(gram))
    for y in range(ROW_Y):
        out_ref[y, PART : PART + SMALL, :] = packed


def forward_first_kernel(count, slots, cols_ref, block_ref, entries_ref, out_ref, tiles_ref):
    for n in range(count * slots):
        tiles_ref[n] = entries_ref[n].astype(f32).astype(bf16)
    forward(cols_ref, block_ref, tiles_ref, out_ref, count, slots)


def forward_second_kernel(count, slots, cols_ref, block_ref, tiles_ref, out_ref):
    forward(cols_ref, block_ref, tiles_ref, out_ref, count, slots)
    square = block_ref[0, PART : PART + SMALL, :]
    for y in range(1, ROW_Y):
        square = square + block_ref[y, PART : PART + SMALL, :]
    out_ref[count * BLOCK : count * BLOCK + SMALL, :] = modp(square)


def over_parts(parts_ref, at):
    total = parts_ref[0, at, :]
    for k in range(1, parts_ref.shape[0]):
        total = total + parts_ref[k, at, :]
    return modp(total)


def backward_first_kernel(count, slots, cols_ref, parts_ref, tiles_ref, out_ref, y_ref, sums_ref):
    projected = []
    for r in range(count):
        at = slice(r * BLOCK, (r + 1) * BLOCK)
        value = over_parts(parts_ref, at)
        y_ref[at, :] = value
        projected.append(value)
    backward(cols_ref, projected, tiles_ref, sums_ref, out_ref, count, slots)


def backward_second_kernel(
    count, slots, cols_ref, parts_ref, tiles_ref, gram_ref, inv_y_ref, out_ref, both_ref, sums_ref
):
    small = slice(count * BLOCK, count * BLOCK + SMALL)
    square = unpack(over_parts(parts_ref, small))
    both = modp(square + gram_ref[...])
    both_ref[...] = both
    projected = []
    for r in range(count):
        at = slice(r * BLOCK, (r + 1) * BLOCK)
        value = over_parts(parts_ref, at)
        projected.append(modp(value - product(both, inv_y_ref[at, :]) + modulus))
    backward(cols_ref, projected, tiles_ref, sums_ref, out_ref, count, slots)


def sum_y_kernel(in_ref, out_ref):
    for z in range(ROW_Z):
        at = slice(z * BLOCK, (z + 1) * BLOCK)
        total = in_ref[0, at, :]
        for y in range(1, ROW_Y):
            total = total + in_ref[y, at, :]
        out_ref[z, :BLOCK, :] = total
    small = slice(PART, PART + SMALL)
    total = in_ref[0, small, :]
    for y in range(1, ROW_Y):
        total = total + in_ref[y, small, :]
    for z in range(ROW_Z):
        out_ref[z, BLOCK:, :] = total


def summed(in_ref):
    total = in_ref[0]
    for k in range(1, in_ref.shape[0]):
        total = total + in_ref[k]
    return modp(total)


def third_kernel(
    gram_ref, square_ref, inverse_ref, older_ref, now_ref, earlier_ref, earliest_ref, out_ref, float_inverse_ref, float_earlier_ref
):
    gram, inverse = gram_ref[...].astype(f32), inverse_ref[...].astype(f32)
    float_inverse_ref[...] = inverse
    float_earlier_ref[...] = earlier_ref[...].astype(f32)
    middle = modp(eye() - product(inverse, gram) + modulus)
    both = modp(square_ref[...].astype(f32) + gram)
    third = product(product(both, middle), older_ref[...].astype(f32))
    out_ref[...] = modp(now_ref[...] - product(third, earliest_ref[...].astype(f32)) + modulus)


def shift_kernel(in_ref, inverse_ref, earlier_ref, base_ref, out_ref, shifted_ref, gram_ref):
    total = summed(in_ref)
    applied = total[:BLOCK]
    gram = unpack(total[BLOCK:])
    gram_ref[...] = gram
    second = product(gram, inverse_ref[...])
    shifted = modp(applied + base_ref[...] + (modulus - product(second, earlier_ref[...])))
    shifted_ref[...] = shifted
    square = pack(self_product(stack_digits(applied)))
    for z in range(ROW_Z):
        out_ref[z, :BLOCK, :] = shifted
        out_ref[z, BLOCK:, :] = square


def spread_y_kernel(in_ref, out_ref):
    square = in_ref[0, BLOCK:, :]
    for z in range(1, ROW_Z):
        square = square + in_ref[z, BLOCK:, :]
    square = modp(square)
    for y in range(ROW_Y):
        for z in range(ROW_Z):
            out_ref[y, z * BLOCK : (z + 1) * BLOCK, :] = in_ref[z, :BLOCK, :]
        out_ref[y, PART:, :] = square


def inverse_kernel(
    count, gram_ref, older_ref, y_ref, now_ref, earlier_ref, inv_y_ref, inv_x_ref, old_ref, inverse_ref
):
    gram = gram_ref[...]
    invert(gram, inverse_ref)
    inverse = inverse_ref[...]
    for r in range(count):
        at = slice(r * BLOCK, (r + 1) * BLOCK)
        inv_y_ref[at, :] = product(inverse, y_ref[at, :])
    inv_x_ref[...] = product(inverse, now_ref[...])
    middle = modp(eye() - product(inverse, gram) + modulus)
    old_ref[...] = product(product(middle, older_ref[...]), earlier_ref[...])


def ending_kernel(
    in_ref, both_ref, shifted_ref, inv_x_ref, old_ref, out_ref, result_ref, base_ref, gram_ref, inverse_ref, inv_next_ref
):
    total = summed(in_ref)
    applied = total[:BLOCK]
    gram = unpack(total[BLOCK:])
    gram_ref[...] = gram
    square = pack(self_product(stack_digits(applied)))
    for k in range(out_ref.shape[0]):
        out_ref[k] = square
    both = both_ref[...]
    following = modp(shifted_ref[...] - product(both, inv_x_ref[...]) + modulus)
    result_ref[...] = following / modulus
    minus = modp(product(gram, inv_x_ref[...]) + product(both, old_ref[...]))
    base_ref[...] = modp(applied + following + (modulus - minus))
    invert(gram, inverse_ref)
    inv_next_ref[...] = product(inverse_ref[...], following)


def relay_kernel(in_ref, out_ref):
    total = summed(in_ref)
    for k in range(out_ref.shape[0]):
        out_ref[k] = total


def last_kernel(in_ref, gram_ref, base_ref, inv_next_ref, out_ref):
    both = modp(unpack(summed(in_ref)) + gram_ref[...])
    out_ref[...] = modp(base_ref[...] - product(both, inv_next_ref[...]) + modulus) / modulus


def exchange(parts, axis):
    return lax.all_to_all(parts, axis, 0, 0, tiled=True)


def flip(x, axis):
    return lax.ppermute(x, axis, [(0, 1), (1, 0)])


def together(*arrays):
    return lax.optimization_barrier(arrays)


def spread_x(part):
    return exchange(jnp.broadcast_to(part[None], (COL_X, *part.shape)), ("x0", "x1"))


def body(entries, tile_cols, block_now, block_prev, block_prev2, gram_prev, square_prev, inverse_prev, inverse_prev2):
    count, slots = tile_cols.shape
    length = count * BLOCK
    stored = entries.reshape(count * slots, TILE, TILE)
    current = block_now.astype(f32)
    shard = (BLOCK, TILE)
    small = (BLOCK, BLOCK)
    sums = [pltpu.VMEM((ROWS, 2 * BLOCK, TILE), f32)]

    along_z = exchange(jnp.broadcast_to(current[None], (ROW_Z, *shard)), Z_LO)
    block = exchange(jnp.broadcast_to(along_z.reshape(1, PART, TILE), (ROW_Y, PART, TILE)), ("y0", "y1"))
    partial, tiles = call(
        functools.partial(forward_first_kernel, count, slots),
        [((length, TILE), f32), (stored.shape, bf16)], [tile_cols, block, stored], smem=(0,),
    )
    other = flip(partial, "zh")
    partial, *given = together(
        partial, gram_prev, square_prev, inverse_prev, inverse_prev2, current, block_prev, block_prev2
    )
    base, inverse_old, earlier = call(
        third_kernel, [(shard, f32), (small, f32), (shard, f32)], given, flops=10**9
    )
    other, base, inverse_old, earlier = together(other, base, inverse_old, earlier)
    pair = partial + other
    parts = spread_x(pair + flip(pair, "c"))

    spread, projected = call(
        functools.partial(backward_first_kernel, count, slots),
        [((ROW_Y, PART + SMALL, TILE), f32), ((length, TILE), f32)],
        [tile_cols, parts, tiles], smem=(0,), scratch=sums,
    )
    chunks = (ROW_Z, BLOCK + SMALL, TILE)
    [by_z] = call(sum_y_kernel, [(chunks, f32)], [exchange(spread, ("y0", "y1"))])
    out, shifted, gram_now = call(
        shift_kernel, [(chunks, f32), (shard, f32), (small, f32)],
        [exchange(by_z, Z_LO), inverse_old, earlier, base],
    )

    [spread] = call(spread_y_kernel, [((ROW_Y, PART + SMALL, TILE), f32)], [exchange(out, Z_LO)])
    [partial] = call(
        functools.partial(forward_second_kernel, count, slots),
        [((length + SMALL, TILE), f32)], [tile_cols, exchange(spread, ("y0", "y1")), tiles], smem=(0,),
    )
    other = flip(partial, "zh")
    partial, gram_now = together(partial, gram_now)
    inv_y, inv_x, old, inverse_now = call(
        functools.partial(inverse_kernel, count),
        [((length, TILE), f32), (shard, f32), (shard, f32), (small, f32)],
        [gram_now, inverse_old, projected, current, earlier],
        flops=10**9,
    )
    other, inv_y, inv_x, old = together(other, inv_y, inv_x, old)
    pair = partial + other
    parts = spread_x(pair + flip(pair, "c"))
    spread, both = call(
        functools.partial(backward_second_kernel, count, slots),
        [((ROW_Y, PART + SMALL, TILE), f32), (small, f32)],
        [tile_cols, parts, tiles, gram_now, inv_y], smem=(0,), scratch=sums,
    )
    [by_z] = call(sum_y_kernel, [(chunks, f32)], [exchange(spread, ("y0", "y1"))])
    near = ROW_Y * COL_X * COL_C
    far = COL_Z * ROW_Z
    out, result, base, gram_next, inverse_next, inv_next = call(
        ending_kernel,
        [((near, SMALL, TILE), f32), (shard, f32), (shard, f32), (small, f32), (small, f32), (shard, f32)],
        [exchange(by_z, Z_LO), both, shifted, inv_x, old],
    )
    [out] = call(relay_kernel, [((far, SMALL, TILE), f32)], [exchange(out, ("y0", "y1", "x0", "x1", "c"))])
    [later] = call(last_kernel, [(shard, f32)], [exchange(out, ("zh", *Z_LO)), gram_next, base, inv_next])
    return result, later


def solution(mesh):
    fine = Mesh(mesh.devices.reshape(2, 2, 2, 2, 2, COL_Z, 2, 2, COL_C), ("z2", "z1", "z0", "y1", "y0", "zh", "x1", "x0", "c"))
    row, col = ("z2", "z1", "z0", "y1", "y0"), ("zh", "x1", "x0", "c")
    columns = P(None, (*col, *row))
    return jax.shard_map(
        body,
        mesh=fine,
        in_specs=(P(row, col, None, None), P(row, col), columns, columns, columns, P(), P(), P(), P()),
        out_specs=(columns, columns),
        check_vma=False,
    )
```
